512 devices in a mesh: gx: 16 (over x, y), gy: 4 (over z_lo), gz: 8 (over z_hi, core).
Axes of the slice: x: 4, y: 4, z: 16 (z_hi: 4, z_lo: 4; z = z_hi * 4 + z_lo), core: 2. Of those that a mesh axis runs over, the one named last changes fastest.
Arguments:
- conc: float32 [1, 128, 256, 1024], P(None, 'gz', 'gx', 'gy'), may hold values from 0.1 to 10
- wind_x: float32 [128, 256, 1024], P('gz', 'gx', 'gy'), may hold values from -0.35 to 0.35
- wind_y: float32 [128, 256, 1024], P('gz', 'gx', 'gy'), may hold values from -0.35 to 0.35
- profiles: float32 [8, 128], replicated, may hold values from 1 to 500
- classes: int32 [256, 1024], P('gx', 'gy'), may hold values from 0 to 7
- heights: int32 [256, 1024], P('gx', 'gy'), may hold values from 0 to 32
- emission: float32 [1, 256, 1024], P(None, 'gx', 'gy'), may hold values from 0.5 to 5
Outputs:
- conc_out: float32 [1, 128, 256, 1024], P(None, 'gz', 'gx', 'gy')
The draws below stay inside these ranges and needn't reach their ends.
All inputs are finite; a program needn't handle non-finite values.
Results may differ from the reference program's by a relative error of at most 0.0003.
Values sent between devices are 32-bit elements; how exact they have to be, the bound alone decides.
No kernel may reach another device: no remote copies, remote signals or barrier semaphores. Data moves between devices by JAX's collectives and lax.ppermute only.
A program may use at most 64 MiB of HBM per device.

```python
import math
import jax
import jax.numpy as jnp
from jax import lax

SPEC = 1
CZ = 16
HSTEPS = 8
NCLASS = 8
NX = 256
NY = 1024
NZ = 128


def draw_conc(key, part):
    base = jax.random.fold_in(key, 11)
    key_x, key_y, key_cell = jax.random.split(base, 3)
    row_x = jnp.exp(jax.random.uniform(key_x, (SPEC, 1, NX, 1), jnp.float32, -0.6, 0.6))
    row_y = jnp.exp(jax.random.uniform(key_y, (SPEC, 1, 1, NY), jnp.float32, -0.6, 0.6))
    cell = jnp.exp(jax.random.uniform(key_cell, (SPEC, NZ, NX, NY), jnp.float32, math.log(0.35), math.log(2.8)))
    return (row_x * row_y * cell).astype(jnp.float32)


def level_winds(key):
    key_sign, key_size = jax.random.split(key, 2)
    order = jax.random.permutation(key_sign, NZ)
    signs = jnp.where(order < NZ // 2, 1.0, -1.0).astype(jnp.float32)[:, None, None]
    size = jax.random.uniform(key_size, (NZ, NX, NY), jnp.float32, 0.25, 0.35)
    return (signs * size).astype(jnp.float32)


def draw_wind_x(key, part):
    return level_winds(jax.random.fold_in(key, 12))


def draw_wind_y(key, part):
    return level_winds(jax.random.fold_in(key, 13))


def touch_ends(drawn, rng, least, high):
    extent = drawn.shape
    index_at = [jax.random.randint(jax.random.fold_in(rng, axis), (), 0, extent[axis]) for axis in range(len(extent))]
    drawn = drawn.at[tuple(index_at)].set(least)
    longest = extent.index(max(extent))
    index_at[longest] = (index_at[longest] + 1) % extent[longest]
    return drawn.at[tuple(index_at)].set(high)


def block_scale(key, shape, cuts, least, top_value):
    level, own = 1.0, jax.random.fold_in(key, 6)
    for axis_at, blocks in cuts:
        steps = jnp.exp(jax.random.uniform(jax.random.fold_in(own, axis_at), (blocks,), jnp.float32, least / len(cuts), top_value / len(cuts)))
        level = level * jnp.repeat(steps, shape[axis_at] // blocks).reshape([-1 if axis == axis_at else 1 for axis in range(len(shape))])
    return level


def setup_inputs(seed: int = 0) -> dict:
    streams_of = jax.random.split(jax.random.key(seed), 8)
    conc = draw_conc(jax.random.fold_in(streams_of[7], 71), 0)
    wind_x = draw_wind_x(jax.random.fold_in(streams_of[7], 71), 0)
    wind_y = draw_wind_y(jax.random.fold_in(streams_of[7], 71), 0)
    profiles = jnp.clip(jnp.exp(jax.random.uniform(streams_of[3], (NCLASS, NZ), jnp.float32, math.log(1.0), math.log(500.0))), 1.0, 500.0)
    classes = touch_ends(jax.random.randint(streams_of[4], (NX, NY), 0, NCLASS), jax.random.fold_in(streams_of[4], 1), 0, NCLASS - 1).astype(jnp.int32)
    heights = touch_ends(jax.random.randint(streams_of[5], (NX, NY), 0, 2 * CZ + 1), jax.random.fold_in(streams_of[5], 1), 0, 2 * CZ).astype(jnp.int32)
    emission = jnp.clip(jnp.exp(math.log(5.0) - 2.3025851 * jax.random.uniform(streams_of[6], (SPEC, NX, NY), jnp.float32) ** block_scale(streams_of[6], (SPEC, NX, NY), ((1, 16), (2, 4)), -0.2, 0.2)), 0.5, 5.0)
    return dict(conc=conc, wind_x=wind_x, wind_y=wind_y, profiles=profiles, classes=classes, heights=heights, emission=emission)


diffusion_number = 0.05
canopy_scale = 0.2

def update(padded, centre, wind_x, wind_y, west_x, south_y):
    east = padded[:, :, 2:, 1:-1]
    west = padded[:, :, :-2, 1:-1]
    north = padded[:, :, 1:-1, 2:]
    south = padded[:, :, 1:-1, :-2]
    flux_east = jnp.maximum(wind_x, 0.0) * centre + jnp.minimum(wind_x, 0.0) * east
    flux_west = jnp.maximum(west_x, 0.0) * west + jnp.minimum(west_x, 0.0) * centre
    flux_north = jnp.maximum(wind_y, 0.0) * centre + jnp.minimum(wind_y, 0.0) * north
    flux_south = jnp.maximum(south_y, 0.0) * south + jnp.minimum(south_y, 0.0) * centre
    spread = east + west + north + south - 4.0 * centre
    return centre - (flux_east - flux_west) - (flux_north - flux_south) + diffusion_number * spread

def reference(conc, wind_x, wind_y, profiles, classes, heights, emission):
    west_x = jnp.pad(wind_x, ((0, 0), (1, 0), (0, 0)))[:, :-1, :]
    south_y = jnp.pad(wind_y, ((0, 0), (0, 0), (1, 0)))[:, :, :-1]
    for step in range(HSTEPS):
        padded = jnp.pad(conc, ((0, 0), (0, 0), (1, 1), (1, 1)))
        conc = update(padded, conc, wind_x, wind_y, west_x, south_y)
    levels = jnp.arange(NZ, dtype=jnp.int32)
    above = jnp.take(profiles, classes, axis=0)
    above = jnp.where(levels[None, None, :] < heights[:, :, None], canopy_scale * above, above)
    below = jnp.pad(above, ((0, 0), (0, 0), (1, 0)))[:, :, :-1]
    diagonal = 1.0 + below + above
    upper = -jnp.where(levels[None, None, :] < NZ - 1, above, jnp.zeros_like(above))
    lower = -below
    rhs = jnp.transpose(conc, (2, 3, 1, 0))
    rhs = rhs.at[:, :, 0, :].add(jnp.transpose(emission, (1, 2, 0)))
    solved = lax.linalg.tridiagonal_solve(lower, diagonal, upper, rhs)
    return jnp.transpose(solved, (3, 2, 0, 1))
```

```python
import jax
import jax.numpy as jnp
from jax import lax
from jax.experimental import pallas as pl
from jax.experimental.pallas import tpu as pltpu
from jax.sharding import PartitionSpec as P

HSTEPS = 8
NCLASS = 8
TILE = 128
DIFFUSION = 0.05
CANOPY = 0.2
LIMIT = 24 * 1024 * 1024

VMEM = pl.BlockSpec(memory_space=pltpu.VMEM)
SMEM = pl.BlockSpec(memory_space=pltpu.SMEM)


def call(kernel, outs, n_smem, scratch, flops):
    return lambda *args: pl.pallas_call(
        kernel,
        out_shape=[jax.ShapeDtypeStruct(s, jnp.float32) for s in outs],
        in_specs=[SMEM] * n_smem + [VMEM] * (len(args) - n_smem),
        out_specs=[VMEM] * len(outs),
        scratch_shapes=[pltpu.VMEM(s, jnp.float32) for s in scratch],
        compiler_params=pltpu.CompilerParams(vmem_limit_bytes=LIMIT),
        cost_estimate=pl.CostEstimate(flops=flops, bytes_accessed=1 << 20, transcendentals=0),
    )(*args)


def pack_kernel(c_ref, wx_ref, wy_ref, lo_ref, hi_ref, yl_ref, yr_ref):
    depth, rows, width = c_ref.shape
    half, strip = rows // 2, HSTEPS
    lane = lax.broadcasted_iota(jnp.int32, (depth, TILE), 1) // strip
    for a, ref in enumerate((c_ref, wx_ref, wy_ref)):
        left = jnp.zeros((depth, TILE), jnp.float32)
        right = left
        for x in range(rows):
            row = ref[:, x, :]
            if x < half:
                lo_ref[a * half + x] = row
            else:
                hi_ref[a * half + x - half] = row
            at = strip * x
            first, last = row[:, :TILE], row[:, width - TILE :]
            if at:
                first = pltpu.roll(first, at, 1)
            if (at + strip) % TILE:
                last = pltpu.roll(last, (at + strip) % TILE, 1)
            left = jnp.where(lane == x, first, left)
            right = jnp.where(lane == x, last, right)
        yl_ref[a] = left
        yr_ref[a] = right


def mixing_kernel(idx_ref, profiles_ref, classes_ref, heights_ref,
                  f_ref, h_ref, g_ref, a_ref, b_ref, w_ref,
                  k_ref, e_ref, d_ref, up_ref, down_ref):
    me = idx_ref[2]
    depth = g_ref.shape[0]
    groups = w_ref.shape[0]
    shape = classes_ref.shape
    total = depth * groups
    classes, heights = classes_ref[...], heights_ref[...]
    bits = [(classes & (1 << b)) != 0 for b in range(3)]

    k_ref[0] = jnp.zeros(shape, jnp.float32)

    def mixing(z, _):
        table = [profiles_ref[c, z] for c in range(NCLASS)]
        for bit in bits:
            table = [jnp.where(bit, table[i + 1], table[i]) for i in range(0, len(table), 2)]
        k = table[0]
        k_ref[z + 1] = jnp.where(z < heights, CANOPY * k, k)
        return 0

    lax.fori_loop(0, total, mixing, 0, unroll=2)

    one = jnp.ones(shape, jnp.float32)

    def chunk(n, carry):
        e, d = carry
        m = groups - 1 - n
        aside_e = jnp.where(n == me, 0, depth)
        aside_d = jnp.where(m == me, 0, depth)

        def level(i, carry):
            e, d, up, down = carry
            k = k_ref[n * depth + i + 1]
            f = k / (e + k)
            f_ref[aside_e + i] = f
            e_ref[aside_e + i] = e
            j = depth - 1 - i
            kb = k_ref[m * depth + j]
            h = kb / (d + kb)
            h_ref[aside_d + j] = h
            d_ref[aside_d + j] = d
            return 1.0 + f * e, 1.0 + h * d, up * f, down * h

        e, d, up, down = lax.fori_loop(0, depth, level, (e, d, one, one))
        up_ref[n] = up
        down_ref[m] = down
        return e, d

    lax.fori_loop(0, groups, chunk, (one, 1.0 + k_ref[total]))

    run = one
    for i in range(depth):
        g = 1.0 / (e_ref[i] + d_ref[i] - 1.0)
        g_ref[i] = g
        a_ref[i] = g * run
        run = run * f_ref[i]
    run = one
    for i in reversed(range(depth)):
        b_ref[i] = g_ref[i] * run
        run = run * h_ref[i]
    zero = jnp.zeros(shape, jnp.float32)
    run = one
    for s in reversed(range(groups)):
        below = s < me
        w_ref[s] = jnp.where(below, run, zero)
        run = jnp.where(below, run * up_ref[s], one)
    run = one
    for s in range(groups):
        above = s > me
        w_ref[s] = w_ref[s] + jnp.where(above, run, zero)
        run = jnp.where(above, run * down_ref[s], one)


def transport_kernel(idx_ref, lo_ref, hi_ref, west_ref, east_ref, f_ref, h_ref, g_ref, emission_ref,
                     u_ref, send_ref, c_ref, k_ref, t_ref):
    gx, gy, me = idx_ref[0], idx_ref[1], idx_ref[2]
    depth, rows, width = u_ref.shape
    groups = send_ref.shape[0]
    half, strip = rows // 2, HSTEPS
    ext = rows + 2 * strip
    wide = width + TILE
    lane = lax.broadcasted_iota(jnp.int32, (depth, TILE), 1)
    n_gx, n_gy = idx_ref[3], idx_ref[4]

    def plane(a, r):
        if r < strip:
            ref, at, group = west_ref, r, half + r
        elif r < strip + half:
            ref, at, group = lo_ref, r - strip, r - strip
        elif r < strip + rows:
            ref, at, group = hi_ref, r - strip - half, r - strip
        else:
            ref, at, group = east_ref, r - strip - rows, r - strip - rows
        side = ref[3 * half + a]
        low, high = side[:, :TILE], side[:, TILE:]
        shift_high = (-strip * group) % TILE
        shift_low = (-strip * (group + 1)) % TILE
        if shift_high:
            high = pltpu.roll(high, shift_high, 1)
        if shift_low:
            low = pltpu.roll(low, shift_low, 1)
        last = jnp.where(lane < strip, high, jnp.where(lane >= TILE - strip, low, 0.0))
        return jnp.concatenate([ref[a * half + at], last], axis=1)

    one = jnp.ones((depth, width), jnp.float32)
    sides = jnp.where((lane < strip) & (gy < n_gy - 1) | (lane >= TILE - strip) & (gy > 0), 1.0, 0.0)
    inside = jnp.concatenate([one, sides], axis=1)
    west_in = inside * jnp.where(gx > 0, 1.0, 0.0)
    east_in = inside * jnp.where(gx < n_gx - 1, 1.0, 0.0)

    c_ref[0] = plane(0, 0)
    c_ref[ext - 1] = plane(0, ext - 1)
    aw = plane(1, 0)
    for r in range(1, ext - 1):
        c_ref[r] = plane(0, r)
        ax, ay = plane(1, r), plane(2, r)
        south = pltpu.roll(ay, 1, 1)
        ax_up, aw_up = jnp.maximum(ax, 0.0), jnp.maximum(aw, 0.0)
        ay_up, as_up = jnp.maximum(ay, 0.0), jnp.maximum(south, 0.0)
        ax_down, aw_down = jnp.minimum(ax, 0.0), jnp.minimum(aw, 0.0)
        ay_down, as_down = jnp.minimum(ay, 0.0), jnp.minimum(south, 0.0)
        own = (1.0 - 4.0 * DIFFUSION) - (ax_up - aw_down) - (ay_up - as_down)
        mask = west_in if r < strip else east_in if r >= strip + rows else inside
        k_ref[0, r] = own * mask
        k_ref[1, r] = (DIFFUSION - ax_down) * mask
        k_ref[2, r] = (DIFFUSION + aw_up) * mask
        k_ref[3, r] = (DIFFUSION - ay_down) * mask
        k_ref[4, r] = (DIFFUSION + as_up) * mask
        aw = ax

    for step in range(1, HSTEPS + 1):

        def row(r, carry):
            west, own = carry
            east = c_ref[r + 1]
            north = pltpu.roll(own, wide - 1, 1)
            south = pltpu.roll(own, 1, 1)
            c_ref[r] = (
                (k_ref[0, r] * own + k_ref[1, r] * east)
                + (k_ref[2, r] * west + k_ref[3, r] * north)
                + k_ref[4, r] * south
            )
            return own, east

        lax.fori_loop(step, ext - step, row, (c_ref[step - 1], c_ref[step]), unroll=2)

    def level(z):
        d = c_ref[strip : strip + rows, z, :width]
        if z == 0:
            d = d + emission_ref[...] * jnp.where(me == 0, 1.0, 0.0)
        return d

    run = None
    for z in range(depth):
        d = level(z)
        run = d if z == 0 else d + f_ref[z - 1] * run
        t_ref[z] = run - d
    beta = f_ref[depth - 1] * run
    run = None
    for z in reversed(range(depth)):
        d = level(z)
        run = d if z == depth - 1 else d + h_ref[z + 1] * run
        u_ref[z] = g_ref[z] * (t_ref[z] + run)
    gamma = h_ref[0] * run
    for s in range(groups):
        send_ref[s] = jnp.where(s > me, beta, gamma)


def finish_kernel(idx_ref, u_ref, a_ref, b_ref, w_ref, got_ref, out_ref):
    me = idx_ref[2]
    depth, rows, width = u_ref.shape
    groups = w_ref.shape[0]
    zero = jnp.zeros((rows, width), jnp.float32)
    below, above = zero, zero
    for s in range(groups):
        term = w_ref[s] * got_ref[s]
        below = below + jnp.where(s < me, term, zero)
        above = above + jnp.where(s > me, term, zero)
    for z in range(depth):
        out_ref[z] = u_ref[z] + (a_ref[z] * below + b_ref[z] * above)


def shifted(x, axis, by):
    length = lax.axis_size(axis)
    return lax.ppermute(x, axis, [(i, i + by) for i in range(length) if 0 <= i + by < length])


def local(conc, wind_x, wind_y, profiles, classes, heights, emission):
    species, depth, rows, width = conc.shape
    groups = lax.axis_size("gz")
    half, ext, wide = rows // 2, rows + 2 * HSTEPS, width + TILE
    idx = jnp.stack(
        [lax.axis_index("gx"), lax.axis_index("gy"), lax.axis_index("gz"),
         jnp.int32(lax.axis_size("gx")), jnp.int32(lax.axis_size("gy"))]
    ).astype(jnp.int32)
    block, pane = (depth, rows, width), (rows, width)
    planes = 3 * half + 3

    lo, hi, left, right = call(
        pack_kernel, [(planes, depth, width)] * 2 + [(3, depth, TILE)] * 2, 0, [], 1 << 20
    )(conc[0], wind_x, wind_y)
    from_south = shifted(right, "gy", 1)
    from_north = shifted(left, "gy", -1)
    side = jnp.concatenate([from_south, from_north], axis=2)
    lo = lax.dynamic_update_slice(lo, side, (3 * half, 0, 0))
    hi = lax.dynamic_update_slice(hi, side, (3 * half, 0, 0))
    west = shifted(hi, "gx", 1)
    east = shifted(lo, "gx", -1)

    twice = (2 * depth, rows, width)
    f, h, g, a, b, w = call(
        mixing_kernel, [twice, twice, block, block, block, (groups, *pane)], 2,
        [(depth * groups + 1, *pane), twice, twice, (groups, *pane), (groups, *pane)], 1 << 26,
    )(idx, profiles, classes, heights)

    u, send = call(
        transport_kernel, [block, (groups, *pane)], 1,
        [(ext, depth, wide), (5, ext, depth, wide), block], 1 << 24,
    )(idx, lo, hi, west, east, f, h, g, emission[0])
    got = lax.all_to_all(send, "gz", split_axis=0, concat_axis=0, tiled=True)
    (out,) = call(finish_kernel, [block], 1, [], 1 << 20)(idx, u, a, b, w, got)
    return out[None]


def solution(mesh):
    return jax.shard_map(
        local,
        mesh=mesh,
        in_specs=(
            P(None, "gz", "gx", "gy"),
            P("gz", "gx", "gy"),
            P("gz", "gx", "gy"),
            P(),
            P("gx", "gy"),
            P("gx", "gy"),
            P(None, "gx", "gy"),
        ),
        out_specs=P(None, "gz", "gx", "gy"),
        check_vma=False,
    )
```

```python
import jax
import jax.numpy as jnp
from jax import lax
from jax.experimental import pallas as pl
from jax.experimental.pallas import tpu as pltpu
from jax.sharding import PartitionSpec as P

HSTEPS = 8
NCLASS = 8
TILE = 128
DIFFUSION = 0.05
CANOPY = 0.2
LIMIT = 10 * 1024 * 1024
PARTS = 4

VMEM = pl.BlockSpec(memory_space=pltpu.VMEM)
SMEM = pl.BlockSpec(memory_space=pltpu.SMEM)
HBM = pl.BlockSpec(memory_space=pltpu.HBM)


def call(kernel, ins, outs, scratch, flops, out_spec=VMEM):
    return pl.pallas_call(
        kernel,
        out_shape=[jax.ShapeDtypeStruct(s, jnp.float32) for s in outs],
        in_specs=ins,
        out_specs=[out_spec] * len(outs),
        scratch_shapes=[pltpu.VMEM(s, jnp.float32) if isinstance(s, tuple) else s for s in scratch],
        compiler_params=pltpu.CompilerParams(vmem_limit_bytes=LIMIT),
        cost_estimate=pl.CostEstimate(flops=flops, bytes_accessed=1 << 20, transcendentals=0),
    )


def pack_kernel(c_hbm, wx_hbm, wy_hbm, own_ref, yl_ref, yr_ref, in_ref, sems):
    depth, rows, width = c_hbm.shape
    half, strip, part = rows // 2, HSTEPS, depth // PARTS
    copies = []
    for a, ref in enumerate((c_hbm, wx_hbm, wy_hbm)):
        for q in range(PARTS):
            at = pl.ds(q * part, part)
            copies.append(pltpu.make_async_copy(ref.at[at], in_ref.at[a, at], sems.at[a * PARTS + q]))
            copies[-1].start()
    lane = lax.broadcasted_iota(jnp.int32, (depth, TILE), 1) // strip
    for a in range(3):
        for q in range(PARTS):
            copies[a * PARTS + q].wait()
        left = jnp.zeros((depth, TILE), jnp.float32)
        right = left
        for x in range(rows):
            row = in_ref[a, :, x, :]
            own_ref[a, x] = row
            first, last = row[:, :TILE], row[:, width - TILE :]
            group = 2 * (x % half)
            to_left, to_right = group + 1 - x // half, group + x // half
            if to_left:
                first = pltpu.roll(first, strip * to_left, 1)
            if (to_right + 1) * strip % TILE:
                last = pltpu.roll(last, (to_right + 1) * strip % TILE, 1)
            left = jnp.where(lane == to_left, first, left)
            right = jnp.where(lane == to_right, last, right)
        yl_ref[a] = left
        yr_ref[a] = right


def send_kernel(own_ref, south_ref, north_ref, lo_ref, hi_ref, side_lo_ref, side_hi_ref):
    _, rows, depth, width = own_ref.shape
    half = rows // 2
    to_lo, to_hi = 0, 0
    for a in range(3):
        for x in range(rows):
            first, last = own_ref[a, x, :, :TILE], own_ref[a, x, :, TILE:]
            if x < half and not (a > 0 and x == half - 1):
                lo_ref[to_lo], lo_ref[to_lo + 1] = first, last
                to_lo += 2
            if x >= half and not (a == 2 and x == half):
                hi_ref[to_hi], hi_ref[to_hi + 1] = first, last
                to_hi += 2
    even = lax.broadcasted_iota(jnp.int32, (depth, TILE), 1) // HSTEPS % 2 == 0
    for a in range(3):
        south, north = south_ref[a], north_ref[a]
        low = jnp.where(even, south, north)
        high = jnp.where(even, pltpu.roll(south, TILE - HSTEPS, 1), pltpu.roll(north, HSTEPS, 1))
        side_lo_ref[a] = low
        side_hi_ref[a] = high
        lo_ref[to_lo + a] = low
        hi_ref[to_hi + a] = high


def table_kernel(profiles_ref, classes_ref, heights_ref, k_ref):
    total = k_ref.shape[0] - 1
    classes, heights = classes_ref[...], heights_ref[...]
    bits = [(classes & (1 << b)) != 0 for b in range(3)]
    k_ref[0] = jnp.zeros(classes.shape, jnp.float32)

    def mixing(z, _):
        table = [profiles_ref[c, z] for c in range(NCLASS)]
        for bit in bits:
            table = [jnp.where(bit, table[i + 1], table[i]) for i in range(0, len(table), 2)]
        k = table[0]
        k_ref[z + 1] = jnp.where(z < heights, CANOPY * k, k)
        return 0

    lax.fori_loop(0, total, mixing, 0, unroll=4)


def factor_kernel(idx_ref, k_ref, f_ref, h_ref, g_ref, a_ref, b_ref, w_ref,
                  e_ref, d_ref, up_ref, down_ref):
    me = idx_ref[2]
    depth = g_ref.shape[0]
    groups = w_ref.shape[0]
    shape = w_ref.shape[1:]
    total = depth * groups
    one = jnp.ones(shape, jnp.float32)

    def chunk(n, carry):
        e, d = carry
        m = groups - 1 - n
        aside_e = jnp.where(n == me, 0, depth)
        aside_d = jnp.where(m == me, 0, depth)

        def level(i, carry):
            e, d, up, down = carry
            k = k_ref[n * depth + i + 1]
            f = k / (e + k)
            f_ref[aside_e + i] = f
            e_ref[aside_e + i] = e
            j = depth - 1 - i
            kb = k_ref[m * depth + j]
            h = kb / (d + kb)
            h_ref[aside_d + j] = h
            d_ref[aside_d + j] = d
            return 1.0 + f * e, 1.0 + h * d, up * f, down * h

        e, d, up, down = lax.fori_loop(0, depth, level, (e, d, one, one))
        up_ref[n] = up
        down_ref[m] = down
        return e, d

    lax.fori_loop(0, groups, chunk, (one, 1.0 + k_ref[total]))

    run = one
    for i in range(depth):
        g = 1.0 / (e_ref[i] + d_ref[i] - 1.0)
        g_ref[i] = g
        a_ref[i] = g * run
        run = run * f_ref[i]
    run = one
    for i in reversed(range(depth)):
        b_ref[i] = g_ref[i] * run
        run = run * h_ref[i]
    zero = jnp.zeros(shape, jnp.float32)
    run = one
    for s in reversed(range(groups)):
        below = s < me
        w_ref[s] = jnp.where(below, run, zero)
        run = jnp.where(below, run * up_ref[s], one)
    run = one
    for s in range(groups):
        above = s > me
        w_ref[s] = w_ref[s] + jnp.where(above, run, zero)
        run = jnp.where(above, run * down_ref[s], one)


def coefficients(ax, aw, ay, mask):
    south = pltpu.roll(ay, 1, 1)
    ax_up, ay_up, as_up = jnp.maximum(ax, 0.0), jnp.maximum(ay, 0.0), jnp.maximum(south, 0.0)
    ax_down, ay_down, as_down = jnp.minimum(ax, 0.0), jnp.minimum(ay, 0.0), jnp.minimum(south, 0.0)
    own = (1.0 - 4.0 * DIFFUSION) - ax_up - (ay_up - as_down)
    west = DIFFUSION
    if aw is not None:
        own = own + jnp.minimum(aw, 0.0)
        west = west + jnp.maximum(aw, 0.0)
    return own * mask, (DIFFUSION - ax_down) * mask, west * mask, (DIFFUSION - ay_down) * mask, (DIFFUSION + as_up) * mask


def substep(k_ref, r, own, east, west):
    north = pltpu.roll(own, own.shape[1] - 1, 1)
    south = pltpu.roll(own, 1, 1)
    return (k_ref[0, r] * own + k_ref[1, r] * east) + (k_ref[2, r] * west + k_ref[3, r] * north) + k_ref[4, r] * south


def with_strips(first, last, side, row):
    by = (TILE - HSTEPS - 2 * HSTEPS * row) % TILE
    return jnp.concatenate([first, last, pltpu.roll(side, by, 1) if by else side], axis=1)


def inside_mask(depth, width, gy, n_gy):
    lane = lax.broadcasted_iota(jnp.int32, (depth, TILE), 1)
    sides = jnp.where((lane < HSTEPS) & (gy < n_gy - 1) | (lane >= TILE - HSTEPS) & (gy > 0), 1.0, 0.0)
    return jnp.concatenate([jnp.ones((depth, width), jnp.float32), sides], axis=1)


def inner_kernel(idx_ref, own_ref, side_lo_ref, side_hi_ref, k_ref, edge_ref, wind_ref, c_ref):
    gy, n_gy = idx_ref[1], idx_ref[4]
    _, rows, depth, width = own_ref.shape
    half = rows // 2
    mask = inside_mask(depth, width, gy, n_gy)

    def plane(a, x):
        side = side_lo_ref[a] if x < half else side_hi_ref[a]
        return with_strips(own_ref[a, x, :, :TILE], own_ref[a, x, :, TILE:], side, x % half)

    aw = None
    for x in range(rows):
        c_ref[0, x] = plane(0, x)
        ax = plane(1, x)
        for i, k in enumerate(coefficients(ax, aw, plane(2, x), mask)):
            k_ref[i, x] = k
        aw = ax
    wind_ref[...] = aw
    for step in range(HSTEPS):
        src = step % 2
        for i, x in enumerate((step, step + 1, rows - 2 - step, rows - 1 - step)):
            edge_ref[step, i] = c_ref[src, x]
        for x in range(step + 1, rows - 1 - step):
            c_ref[1 - src, x] = substep(k_ref, x, c_ref[src, x], c_ref[src, x + 1], c_ref[src, x - 1])


def outer_kernel(idx_ref, west_ref, east_ref, inner_ref, edge_ref, wind_ref, f_ref, h_ref, g_ref, emission_ref,
                 u_ref, send_ref, c_ref, k_ref, t_ref):
    gx, gy, me = idx_ref[0], idx_ref[1], idx_ref[2]
    n_gx, n_gy = idx_ref[3], idx_ref[4]
    depth, rows, width = u_ref.shape
    groups = send_ref.shape[0]
    half, strip = rows // 2, HSTEPS
    ext = rows + 2 * strip
    inside = inside_mask(depth, width, gy, n_gy)
    west_in = inside * jnp.where(gx > 0, 1.0, 0.0)
    east_in = inside * jnp.where(gx < n_gx - 1, 1.0, 0.0)

    def west_plane(a, r):
        at = 2 * (half * a + r - (a == 2))
        return with_strips(west_ref[at], west_ref[at + 1], west_ref[6 * half - 2 + a], r)

    def east_plane(a, r):
        at = 2 * (half * a + r - (a == 2))
        return with_strips(east_ref[at], east_ref[at + 1], east_ref[6 * half - 4 + a], r)

    aw = west_plane(1, 0)
    c_ref[0, 0] = west_plane(0, 0)
    for r in range(1, strip):
        c_ref[0, r] = west_plane(0, r)
        ax = west_plane(1, r)
        for i, k in enumerate(coefficients(ax, aw, west_plane(2, r), west_in)):
            k_ref[i, r] = k
        aw = ax
    for i in range(5):
        k = inner_ref[i, 0]
        if i == 0:
            k = k + jnp.minimum(aw, 0.0) * inside
        if i == 2:
            k = k + jnp.maximum(aw, 0.0) * inside
        k_ref[i, strip] = k
    aw = wind_ref[...]
    for r in range(strip - 1):
        c_ref[0, strip + rows + r] = east_plane(0, r)
        ax = east_plane(1, r)
        for i, k in enumerate(coefficients(ax, aw, east_plane(2, r), east_in)):
            k_ref[i, strip + rows + r] = k
        aw = ax
    c_ref[0, ext - 1] = east_plane(0, strip - 1)

    for step in range(1, strip + 1):
        src = (step - 1) % 2
        for i in range(strip):
            for r, side in ((step + i, 0), (ext - 1 - step - i, 1)):
                low_side = side == 0
                def at(q):
                    if low_side and q >= strip - 1 + step:
                        return edge_ref[step - 1, q - (strip - 1 + step)]
                    if not low_side and q <= strip + rows - step:
                        return edge_ref[step - 1, q - (strip + rows - step) + 3]
                    return c_ref[src, q]
                weights = k_ref if r <= strip or r >= strip + rows else inner_ref
                row = r if weights is k_ref else r - strip
                new = substep(weights, row, at(r), at(r + 1), at(r - 1))
                if step < strip:
                    c_ref[1 - src, r] = new
                else:
                    c_ref[1 - src, r, :, :width] = new[:, :width]
    last = strip % 2

    def level(z):
        d = c_ref[last, strip : strip + rows, z, :width]
        if z == 0:
            d = d + emission_ref[...] * jnp.where(me == 0, 1.0, 0.0)
        return d

    run = None
    for z in range(depth):
        d = level(z)
        run = d if z == 0 else d + f_ref[z - 1] * run
        t_ref[z] = run - d
    beta = f_ref[depth - 1] * run
    run = None
    for z in reversed(range(depth)):
        d = level(z)
        run = d if z == depth - 1 else d + h_ref[z + 1] * run
        u_ref[z] = g_ref[z] * (t_ref[z] + run)
    gamma = h_ref[0] * run
    for s in range(groups):
        send_ref[s] = jnp.where(s > me, beta, gamma)


def finish_kernel(idx_ref, u_ref, a_ref, b_ref, w_ref, got_ref, out_hbm, out_ref, sems):
    me = idx_ref[2]
    depth, rows, width = u_ref.shape
    groups = w_ref.shape[0]
    part = depth // PARTS
    zero = jnp.zeros((rows, width), jnp.float32)
    below, above = zero, zero
    for s in range(groups):
        term = w_ref[s] * got_ref[s]
        below = below + jnp.where(s < me, term, zero)
        above = above + jnp.where(s > me, term, zero)
    copies = []
    for q in range(PARTS):
        for z in range(q * part, (q + 1) * part):
            out_ref[z] = u_ref[z] + (a_ref[z] * below + b_ref[z] * above)
        at = pl.ds(q * part, part)
        copies.append(pltpu.make_async_copy(out_ref.at[at], out_hbm.at[at], sems.at[q]))
        copies[-1].start()
    for copy in copies:
        copy.wait()


def shifted(x, axis, by):
    length = lax.axis_size(axis)
    return lax.ppermute(x, axis, [(i, i + by) for i in range(length) if 0 <= i + by < length])


def local(conc, wind_x, wind_y, profiles, classes, heights, emission):
    species, depth, rows, width = conc.shape
    groups = lax.axis_size("gz")
    half, ext, wide = rows // 2, rows + 2 * HSTEPS, width + TILE
    idx = jnp.stack(
        [lax.axis_index("gx"), lax.axis_index("gy"), lax.axis_index("gz"),
         jnp.int32(lax.axis_size("gx")), jnp.int32(lax.axis_size("gy"))]
    ).astype(jnp.int32)
    block, pane, tile, row = (depth, rows, width), (rows, width), (depth, TILE), (depth, wide)
    n_lo, n_hi = 6 * half - 4, 6 * half - 2

    own, left, right = call(
        pack_kernel, [HBM] * 3, [(3, rows, depth, width), (3, *tile), (3, *tile)],
        [(3, *block), pltpu.SemaphoreType.DMA((3 * PARTS,))], 1 << 20,
    )(*(pltpu.with_memory_space_constraint(x, pltpu.HBM) for x in (conc[0], wind_x, wind_y)))
    south = shifted(right, "gy", 1)
    north = shifted(left, "gy", -1)
    (k,) = call(table_kernel, [SMEM, VMEM, VMEM], [(depth * groups + 1, *pane)], [], 1 << 24)(
        profiles, classes, heights
    )
    own, south, north, k = lax.optimization_barrier((own, south, north, k))
    lo, hi, side_lo, side_hi = call(
        send_kernel, [VMEM] * 3, [(n_lo + 3, *tile), (n_hi + 3, *tile), (3, *tile), (3, *tile)], [], 1 << 20
    )(own, south, north)
    west = shifted(hi, "gx", 1)
    east = shifted(lo, "gx", -1)
    weights, edge, wind = call(
        inner_kernel, [SMEM] + [VMEM] * 3,
        [(5, rows, *row), (HSTEPS, 4, *row), row], [(2, rows, *row)], 1 << 24,
    )(idx, own, side_lo, side_hi)
    twice = (2 * depth, rows, width)
    f, h, g, a, b, w = call(
        factor_kernel, [SMEM, VMEM], [twice, twice, block, block, block, (groups, *pane)],
        [twice, twice, (groups, *pane), (groups, *pane)], 1 << 24,
    )(idx, k)
    u, send = call(
        outer_kernel, [SMEM] + [VMEM] * 9, [block, (groups, *pane)],
        [(2, ext, *row), (5, ext, *row), block], 1 << 24,
    )(idx, west, east, weights, edge, wind, f, h, g, emission[0])
    got = lax.all_to_all(send, "gz", split_axis=0, concat_axis=0, tiled=True)
    (out,) = call(
        finish_kernel, [SMEM] + [VMEM] * 5, [block], [block, pltpu.SemaphoreType.DMA((PARTS,))], 1 << 20, HBM
    )(idx, u, a, b, w, got)
    return out[None]


def solution(mesh):
    return jax.shard_map(
        local,
        mesh=mesh,
        in_specs=(
            P(None, "gz", "gx", "gy"),
            P("gz", "gx", "gy"),
            P("gz", "gx", "gy"),
            P(),
            P("gx", "gy"),
            P("gx", "gy"),
            P(None, "gx", "gy"),
        ),
        out_specs=P(None, "gz", "gx", "gy"),
        check_vma=False,
    )
```

```python
import functools

import jax
import jax.numpy as jnp
from jax import lax
from jax.experimental import pallas as pl
from jax.experimental.pallas import tpu as pltpu
from jax.sharding import PartitionSpec as P

HSTEPS = 8
NCLASS = 8
TILE = 128
DIFFUSION = 0.05
CANOPY = 0.2
LIMIT = 8 * 1024 * 1024
PARTS = 4

VMEM = pl.BlockSpec(memory_space=pltpu.VMEM)
SMEM = pl.BlockSpec(memory_space=pltpu.SMEM)
HBM = pl.BlockSpec(memory_space=pltpu.HBM)


def call(kernel, ins, outs, scratch, flops, out_spec=VMEM):
    return pl.pallas_call(
        kernel,
        out_shape=[jax.ShapeDtypeStruct(s, jnp.float32) if isinstance(s, tuple) else s for s in outs],
        in_specs=ins,
        out_specs=[out_spec] * len(outs),
        scratch_shapes=[pltpu.VMEM(s, jnp.float32) if isinstance(s, tuple) else s for s in scratch],
        compiler_params=pltpu.CompilerParams(vmem_limit_bytes=LIMIT),
        cost_estimate=pl.CostEstimate(flops=flops, bytes_accessed=1 << 20, transcendentals=0),
    )


def pack_kernel(c_hbm, wx_hbm, wy_hbm, *refs):
    small, (own_ref, yl_ref, yr_ref), kept, (in_ref, sems, small_sems) = refs[:4], refs[4:7], refs[7:11], refs[11:]
    depth, rows, width = c_hbm.shape
    half, strip, part = rows // 2, HSTEPS, depth // PARTS
    copies = []
    for a, ref in enumerate((c_hbm, wx_hbm, wy_hbm)):
        for q in range(PARTS):
            at = pl.ds(q * part, part)
            copies.append(pltpu.make_async_copy(ref.at[at], in_ref.at[a, at], sems.at[a * PARTS + q]))
            copies[-1].start()
    others = [pltpu.make_async_copy(s, d, small_sems.at[i]) for i, (s, d) in enumerate(zip(small, kept))]
    for copy in others:
        copy.start()
    lane = lax.broadcasted_iota(jnp.int32, (depth, TILE), 1) // strip
    for a in range(3):
        for q in range(PARTS):
            copies[a * PARTS + q].wait()
        left = jnp.zeros((depth, TILE), jnp.float32)
        right = left
        for x in range(rows):
            row = in_ref[a, :, x, :]
            own_ref[a, x] = row
            first, last = row[:, :TILE], row[:, width - TILE :]
            group = 2 * (x % half)
            to_left, to_right = group + 1 - x // half, group + x // half
            if to_left:
                first = pltpu.roll(first, strip * to_left, 1)
            if (to_right + 1) * strip % TILE:
                last = pltpu.roll(last, (to_right + 1) * strip % TILE, 1)
            left = jnp.where(lane == to_left, first, left)
            right = jnp.where(lane == to_right, last, right)
        yl_ref[a] = left
        yr_ref[a] = right
    for copy in others:
        copy.wait()


def send_kernel(own_ref, south_ref, north_ref, lo_ref, hi_ref, side_lo_ref, side_hi_ref):
    _, rows, depth, width = own_ref.shape
    half = rows // 2
    to_lo, to_hi = 0, 0
    for a in range(3):
        for x in range(rows):
            if x < half and not (a > 0 and x == half - 1):
                lo_ref[to_lo] = own_ref[a, x]
                to_lo += 1
            if x >= half and not (a == 2 and x == half):
                hi_ref[to_hi] = own_ref[a, x]
                to_hi += 1
    even = lax.broadcasted_iota(jnp.int32, (depth, TILE), 1) // HSTEPS % 2 == 0
    for a in range(3):
        south, north = south_ref[a], north_ref[a]
        low = jnp.where(even, south, north)
        high = jnp.where(even, pltpu.roll(south, TILE - HSTEPS, 1), pltpu.roll(north, HSTEPS, 1))
        side_lo_ref[a] = low
        side_hi_ref[a] = high
        lanes = pl.ds(a % 2 * TILE, TILE)
        lo_ref[to_lo + a // 2, :, lanes] = low
        hi_ref[to_hi + a // 2, :, lanes] = high


def table_kernel(profiles_ref, classes_ref, heights_ref, k_ref):
    total = k_ref.shape[0] - 1
    classes, heights = classes_ref[...], heights_ref[...]
    bits = [(classes & (1 << b)) != 0 for b in range(3)]
    k_ref[0] = jnp.zeros(classes.shape, jnp.float32)

    def mixing(z, _):
        table = [profiles_ref[c, z] for c in range(NCLASS)]
        for bit in bits:
            table = [jnp.where(bit, table[i + 1], table[i]) for i in range(0, len(table), 2)]
        k = table[0]
        k_ref[z + 1] = jnp.where(z < heights, CANOPY * k, k)
        return 0

    lax.fori_loop(0, total, mixing, 0, unroll=4)


def factor_kernel(idx_ref, k_ref, f_ref, h_ref, g_ref, a_ref, b_ref, w_ref,
                  e_ref, d_ref, up_ref, down_ref):
    me = idx_ref[2]
    depth = g_ref.shape[0]
    groups = w_ref.shape[0]
    shape = w_ref.shape[1:]
    total = depth * groups
    one = jnp.ones(shape, jnp.float32)

    def chunk(n, carry):
        e, d = carry
        m = groups - 1 - n
        aside_e = jnp.where(n == me, 0, depth)
        aside_d = jnp.where(m == me, 0, depth)

        def level(i, carry):
            e, d, up, down = carry
            k = k_ref[n * depth + i + 1]
            f = k / (e + k)
            f_ref[aside_e + i] = f
            e_ref[aside_e + i] = e
            j = depth - 1 - i
            kb = k_ref[m * depth + j]
            h = kb / (d + kb)
            h_ref[aside_d + j] = h
            d_ref[aside_d + j] = d
            return 1.0 + f * e, 1.0 + h * d, up * f, down * h

        e, d, up, down = lax.fori_loop(0, depth, level, (e, d, one, one))
        up_ref[n] = up
        down_ref[m] = down
        return e, d

    lax.fori_loop(0, groups, chunk, (one, 1.0 + k_ref[total]))

    run = one
    for i in range(depth):
        g = 1.0 / (e_ref[i] + d_ref[i] - 1.0)
        g_ref[i] = g
        a_ref[i] = g * run
        run = run * f_ref[i]
    run = one
    for i in reversed(range(depth)):
        b_ref[i] = g_ref[i] * run
        run = run * h_ref[i]
    zero = jnp.zeros(shape, jnp.float32)
    run = one
    for s in reversed(range(groups)):
        below = s < me
        w_ref[s] = jnp.where(below, run, zero)
        run = jnp.where(below, run * up_ref[s], one)
    run = one
    for s in range(groups):
        above = s > me
        w_ref[s] = w_ref[s] + jnp.where(above, run, zero)
        run = jnp.where(above, run * down_ref[s], one)


def coefficients(ax, aw, ay, mask):
    south = pltpu.roll(ay, 1, 1)
    ax_up, ay_up, as_up = jnp.maximum(ax, 0.0), jnp.maximum(ay, 0.0), jnp.maximum(south, 0.0)
    ax_down, ay_down, as_down = jnp.minimum(ax, 0.0), jnp.minimum(ay, 0.0), jnp.minimum(south, 0.0)
    own = (1.0 - 4.0 * DIFFUSION) - ax_up - (ay_up - as_down)
    west = DIFFUSION
    if aw is not None:
        own = own + jnp.minimum(aw, 0.0)
        west = west + jnp.maximum(aw, 0.0)
    return own * mask, (DIFFUSION - ax_down) * mask, west * mask, (DIFFUSION - ay_down) * mask, (DIFFUSION + as_up) * mask


def substep(k_ref, r, own, east, west):
    north = pltpu.roll(own, own.shape[1] - 1, 1)
    south = pltpu.roll(own, 1, 1)
    return (k_ref[0, r] * own + k_ref[1, r] * east) + (k_ref[2, r] * west + k_ref[3, r] * north) + k_ref[4, r] * south


def with_strips(cells, side, row):
    by = (TILE - HSTEPS - 2 * HSTEPS * row) % TILE
    return jnp.concatenate([cells, pltpu.roll(side, by, 1) if by else side], axis=1)


def inside_mask(depth, width, gy, n_gy):
    lane = lax.broadcasted_iota(jnp.int32, (depth, TILE), 1)
    sides = jnp.where((lane < HSTEPS) & (gy < n_gy - 1) | (lane >= TILE - HSTEPS) & (gy > 0), 1.0, 0.0)
    return jnp.concatenate([jnp.ones((depth, width), jnp.float32), sides], axis=1)


def inner_kernel(idx_ref, own_ref, side_lo_ref, side_hi_ref, k_ref, edge_ref, wind_ref, c_ref):
    gy, n_gy = idx_ref[1], idx_ref[4]
    _, rows, depth, width = own_ref.shape
    half = rows // 2
    mask = inside_mask(depth, width, gy, n_gy)

    def plane(a, x):
        side = side_lo_ref[a] if x < half else side_hi_ref[a]
        return with_strips(own_ref[a, x], side, x % half)

    aw = None
    for x in range(rows):
        c_ref[0, x] = plane(0, x)
        ax = plane(1, x)
        for i, k in enumerate(coefficients(ax, aw, plane(2, x), mask)):
            k_ref[i, x] = k
        aw = ax
    wind_ref[...] = aw
    for step in range(HSTEPS):
        src = step % 2
        for i, x in enumerate((step, step + 1, rows - 2 - step, rows - 1 - step)):
            edge_ref[step, i] = c_ref[src, x]
        for x in range(step + 1, rows - 1 - step):
            c_ref[1 - src, x] = substep(k_ref, x, c_ref[src, x], c_ref[src, x + 1], c_ref[src, x - 1])


def outer_kernel(low, idx_ref, got_ref, inner_ref, edge_ref, wind_ref, f_ref, h_ref, g_ref, emission_ref,
                 u_ref, send_ref, c_ref, k_ref, t_ref):
    gx, gy, me = idx_ref[0], idx_ref[1], idx_ref[2]
    n_gx, n_gy = idx_ref[3], idx_ref[4]
    depth, half, width = u_ref.shape
    groups = send_ref.shape[0]
    strip = HSTEPS
    inside = inside_mask(depth, width, gy, n_gy)
    halo_in = inside * jnp.where(gx > 0 if low else gx < n_gx - 1, 1.0, 0.0)
    n_got = 3 * half - (1 if low else 2)

    def plane(a, r):
        side = got_ref[n_got + a // 2, :, pl.ds(a % 2 * TILE, TILE)]
        return with_strips(got_ref[half * a + r - (a == 2)], side, r)

    first = 0 if low else half + 1
    aw = plane(1, 0) if low else wind_ref[...]
    if low:
        c_ref[0, 0] = plane(0, 0)
    else:
        c_ref[0, first + strip - 1] = plane(0, strip - 1)
    for r in range(1, strip) if low else range(strip - 1):
        c_ref[0, first + r] = plane(0, r)
        ax = plane(1, r)
        for i, k in enumerate(coefficients(ax, aw, plane(2, r), halo_in)):
            k_ref[i, r] = k
        aw = ax
    if low:
        for i in range(5):
            k = inner_ref[i, 0]
            if i == 0:
                k = k + jnp.minimum(aw, 0.0) * inside
            if i == 2:
                k = k + jnp.maximum(aw, 0.0) * inside
            k_ref[i, strip] = k

    for step in range(1, strip + 1):
        src = (step - 1) % 2
        reach = strip - 1 + step if low else half + 1 - step

        def at(q):
            if low and q >= reach:
                return edge_ref[step - 1, q - reach]
            if not low and q <= reach:
                return edge_ref[step - 1, q - reach + 3]
            return c_ref[src, q]

        for i in range(strip):
            r = (step if low else reach) + i
            if low:
                weights, row = (k_ref, r) if r <= strip else (inner_ref, r - strip)
            else:
                weights, row = (k_ref, r - first) if r >= first else (inner_ref, r + half - 1)
            new = substep(weights, row, at(r), at(r + 1), at(r - 1))
            if step < strip:
                c_ref[1 - src, r] = new
            else:
                c_ref[1 - src, r, :, :width] = new[:, :width]
    last = strip % 2
    begin = strip if low else 1

    def level(z):
        d = c_ref[last, begin : begin + half, z, :width]
        if z == 0:
            mine = emission_ref[:half] if low else emission_ref[half:]
            d = d + mine * jnp.where(me == 0, 1.0, 0.0)
        return d

    mine = pl.ds(0 if low else half, half)
    run = None
    for z in range(depth):
        d = level(z)
        run = d if z == 0 else d + f_ref[z - 1, mine] * run
        t_ref[z] = run - d
    beta = f_ref[depth - 1, mine] * run
    run = None
    for z in reversed(range(depth)):
        d = level(z)
        run = d if z == depth - 1 else d + h_ref[z + 1, mine] * run
        u_ref[z] = g_ref[z, mine] * (t_ref[z] + run)
    gamma = h_ref[0, mine] * run
    for s in range(groups):
        send_ref[s] = jnp.where(s > me, beta, gamma)


def finish_kernel(idx_ref, west_ref, east_ref, a_ref, b_ref, w_ref, got_ref, out_hbm, out_ref, sems):
    me = idx_ref[2]
    depth, rows, width = a_ref.shape
    groups, half, part = w_ref.shape[0], rows // 2, depth // PARTS
    zero = jnp.zeros((rows, width), jnp.float32)
    below, above = zero, zero
    for s in range(groups):
        term = w_ref[s] * got_ref[s]
        below = below + jnp.where(s < me, term, zero)
        above = above + jnp.where(s > me, term, zero)
    copies = []
    for q in range(PARTS):
        for z in range(q * part, (q + 1) * part):
            more = a_ref[z] * below + b_ref[z] * above
            out_ref[z, :half] = west_ref[z] + more[:half]
            out_ref[z, half:] = east_ref[z] + more[half:]
        at = pl.ds(q * part, part)
        copies.append(pltpu.make_async_copy(out_ref.at[at], out_hbm.at[at], sems.at[q]))
        copies[-1].start()
    for copy in copies:
        copy.wait()


def shifted(x, axis, by):
    length = lax.axis_size(axis)
    return lax.ppermute(x, axis, [(i, i + by) for i in range(length) if 0 <= i + by < length])


def local(conc, wind_x, wind_y, profiles, classes, heights, emission):
    species, depth, rows, width = conc.shape
    groups = lax.axis_size("gz")
    half, wide = rows // 2, width + TILE
    idx = jnp.stack(
        [lax.axis_index("gx"), lax.axis_index("gy"), lax.axis_index("gz"),
         jnp.int32(lax.axis_size("gx")), jnp.int32(lax.axis_size("gy"))]
    ).astype(jnp.int32)
    block, pane, tile, row = (depth, rows, width), (rows, width), (depth, TILE), (depth, wide)
    n_lo, n_hi = 3 * half - 2, 3 * half - 1

    small = (profiles, classes, heights, emission[0])
    own, left, right, profiles, classes, heights, emission = call(
        pack_kernel, [HBM] * 7,
        [(3, rows, depth, width), (3, *tile), (3, *tile), *(jax.ShapeDtypeStruct(x.shape, x.dtype) for x in small)],
        [(3, *block), pltpu.SemaphoreType.DMA((3 * PARTS,)), pltpu.SemaphoreType.DMA((len(small),))], 1 << 20,
    )(*(pltpu.with_memory_space_constraint(x, pltpu.HBM) for x in (conc[0], wind_x, wind_y, *small)))
    south = shifted(right, "gy", 1)
    north = shifted(left, "gy", -1)
    (k,) = call(table_kernel, [SMEM, VMEM, VMEM], [(depth * groups + 1, *pane)], [], 1 << 24)(
        profiles, classes, heights
    )
    own, south, north, k = lax.optimization_barrier((own, south, north, k))
    lo, hi, side_lo, side_hi = call(
        send_kernel, [VMEM] * 3,
        [(n_lo + 2, depth, width), (n_hi + 2, depth, width), (3, *tile), (3, *tile)], [], 1 << 20
    )(own, south, north)
    west = shifted(hi, "gx", 1)
    east = shifted(lo, "gx", -1)
    weights, edge, wind = call(
        inner_kernel, [SMEM] + [VMEM] * 3,
        [(5, rows, *row), (HSTEPS, 4, *row), row], [(2, rows, *row)], 1 << 24,
    )(idx, own, side_lo, side_hi)
    twice = (2 * depth, rows, width)
    f, h, g, a, b, w = call(
        factor_kernel, [SMEM, VMEM], [twice, twice, block, block, block, (groups, *pane)],
        [twice, twice, (groups, *pane), (groups, *pane)], 1 << 24,
    )(idx, k)
    halves = []
    for low, got in ((True, west), (False, east)):
        if not low:
            wind, _ = lax.optimization_barrier((wind, halves[0][1]))
        halves.append(call(
            functools.partial(outer_kernel, low), [SMEM] + [VMEM] * 8,
            [(depth, half, width), (groups, half, width)],
            [(2, half + HSTEPS + 1, *row), (5, HSTEPS + 1, *row), (depth, half, width)], 1 << 24,
        )(idx, got, weights, edge, wind, f, h, g, emission))
    send = jnp.concatenate([s for _, s in halves], axis=1)
    got = lax.all_to_all(send, "gz", split_axis=0, concat_axis=0, tiled=True)
    (out,) = call(
        finish_kernel, [SMEM] + [VMEM] * 6, [block], [block, pltpu.SemaphoreType.DMA((PARTS,))], 1 << 20, HBM
    )(idx, *(u for u, _ in halves), a, b, w, got)
    return out[None]


def solution(mesh):
    return jax.shard_map(
        local,
        mesh=mesh,
        in_specs=(
            P(None, "gz", "gx", "gy"),
            P("gz", "gx", "gy"),
            P("gz", "gx", "gy"),
            P(),
            P("gx", "gy"),
            P("gx", "gy"),
            P(None, "gx", "gy"),
        ),
        out_specs=P(None, "gz", "gx", "gy"),
        check_vma=False,
    )
```

```python
import functools

import jax
import jax.numpy as jnp
from jax import lax
from jax.experimental import pallas as pl
from jax.experimental.pallas import tpu as pltpu
from jax.sharding import PartitionSpec as P

HSTEPS = 8
NCLASS = 8
TILE = 128
DIFFUSION = 0.05
CANOPY = 0.2
LIMIT = 8 * 1024 * 1024
PARTS = 1
LEVELS = 8

VMEM = pl.BlockSpec(memory_space=pltpu.VMEM)
SMEM = pl.BlockSpec(memory_space=pltpu.SMEM)
HBM = pl.BlockSpec(memory_space=pltpu.HBM)


def call(kernel, ins, outs, scratch, flops, out_spec=VMEM):
    return pl.pallas_call(
        kernel,
        out_shape=[jax.ShapeDtypeStruct(s, jnp.float32) if isinstance(s, tuple) else s for s in outs],
        in_specs=ins,
        out_specs=[out_spec] * len(outs),
        scratch_shapes=[pltpu.VMEM(s, jnp.float32) if isinstance(s, tuple) else s for s in scratch],
        compiler_params=pltpu.CompilerParams(vmem_limit_bytes=LIMIT),
        cost_estimate=pl.CostEstimate(flops=flops, bytes_accessed=1 << 20, transcendentals=0),
    )


def pack_kernel(idx_ref, c_hbm, wx_hbm, wy_hbm, *refs):
    small, (own_ref, yl_ref, yr_ref), kept, (in_ref, sems, small_sems) = refs[:4], refs[4:7], refs[7:11], refs[11:]
    depth, rows, width = c_hbm.shape
    half, strip, part = rows // 2, HSTEPS, depth // PARTS
    copies = []
    for a, ref in enumerate((c_hbm, wx_hbm, wy_hbm)):
        for q in range(PARTS):
            at = pl.ds(q * part, part)
            copies.append(pltpu.make_async_copy(ref.at[at], in_ref.at[a, at], sems.at[a * PARTS + q]))
            copies[-1].start()
    others = [pltpu.make_async_copy(s, d, small_sems.at[i]) for i, (s, d) in enumerate(zip(small, kept))]
    for copy in others:
        copy.start()
    lane = lax.broadcasted_iota(jnp.int32, (depth, TILE), 1) // strip
    for a in range(3):
        for q in range(PARTS):
            copies[a * PARTS + q].wait()
        left = jnp.zeros((depth, TILE), jnp.float32)
        right = left
        for x in range(rows):
            row = in_ref[a, :, x, :]
            own_ref[a, x] = row
            first, last = row[:, :TILE], row[:, width - TILE :]
            group = 2 * (x % half)
            to_left, to_right = group + 1 - x // half, group + x // half
            if to_left:
                first = pltpu.roll(first, strip * to_left, 1)
            if (to_right + 1) * strip % TILE:
                last = pltpu.roll(last, (to_right + 1) * strip % TILE, 1)
            left = jnp.where(lane == to_left, first, left)
            right = jnp.where(lane == to_right, last, right)
        yl_ref[a] = left
        yr_ref[a] = right
    for copy in others:
        copy.wait()


def send_kernel(own_ref, south_ref, north_ref, lo_ref, hi_ref, side_lo_ref, side_hi_ref):
    _, rows, depth, width = own_ref.shape
    half = rows // 2
    to_lo, to_hi = 0, 0
    for a in range(3):
        for x in range(rows):
            if x < half and not (a > 0 and x == half - 1):
                lo_ref[to_lo] = own_ref[a, x]
                to_lo += 1
            if x >= half and not (a == 2 and x == half):
                hi_ref[to_hi] = own_ref[a, x]
                to_hi += 1
    even = lax.broadcasted_iota(jnp.int32, (depth, TILE), 1) // HSTEPS % 2 == 0
    for a in range(3):
        south, north = south_ref[a], north_ref[a]
        low = jnp.where(even, south, north)
        high = jnp.where(even, pltpu.roll(south, TILE - HSTEPS, 1), pltpu.roll(north, HSTEPS, 1))
        side_lo_ref[a] = low
        side_hi_ref[a] = high
        lanes = pl.ds(a % 2 * TILE, TILE)
        lo_ref[to_lo + a // 2, :, lanes] = low
        hi_ref[to_hi + a // 2, :, lanes] = high


def table_kernel(profiles_ref, classes_ref, heights_ref, k_ref):
    total = k_ref.shape[0] - 1
    classes, heights = classes_ref[...], heights_ref[...]
    bits = [(classes & (1 << b)) != 0 for b in range(3)]
    k_ref[0] = jnp.zeros(classes.shape, jnp.float32)

    def mixing(z, _):
        table = [profiles_ref[c, z] for c in range(NCLASS)]
        for bit in bits:
            table = [jnp.where(bit, table[i + 1], table[i]) for i in range(0, len(table), 2)]
        k = table[0]
        k_ref[z + 1] = jnp.where(z < heights, CANOPY * k, k)
        return 0

    lax.fori_loop(0, total, mixing, 0, unroll=4)


def factor_kernel(idx_ref, k_ref, f_ref, h_ref, g_ref, a_ref, b_ref, w_ref,
                  n_ref, m_ref, p_ref, q_ref, up_ref, down_ref):
    me = idx_ref[2]
    depth = g_ref.shape[0]
    groups = w_ref.shape[0]
    shape = w_ref.shape[1:]
    total = depth * groups
    one = jnp.ones(shape, jnp.float32)

    def some(t, carry):
        n, p, up, down = carry
        low = t * LEVELS
        high = total - 1 - low
        chunk_n, chunk_p = low // depth, high // depth
        at_n = low % depth + jnp.where(chunk_n == me, 0, depth)
        at_p = high % depth + jnp.where(chunk_p == me, 0, depth)
        m, q = one, one
        for i in range(LEVELS):
            k, kb = k_ref[low + i + 1], k_ref[high - i]
            n_ref[at_n + i], m_ref[at_n + i] = n, m
            p_ref[at_p - i], q_ref[at_p - i] = p, q
            m, q = n + k * m, p + kb * q
            n, p = m + k * n, q + kb * p
            up, down = up * k, down * kb
        m, q = 1.0 / m, 1.0 / q
        up, down = up * m, down * q
        up_ref[chunk_n], down_ref[chunk_p] = up, down
        fresh = low % depth + LEVELS == depth
        return n * m, p * q, jnp.where(fresh, one, up), jnp.where(fresh, one, down)

    lax.fori_loop(0, total // LEVELS, some, (one, 1.0 + k_ref[total], one, one))

    begin = me * depth
    for i in range(depth):
        m, q = m_ref[i], q_ref[i]
        k, kb = k_ref[begin + i + 1], k_ref[begin + i]
        f_ref[i] = k * m / (n_ref[i] + k * m)
        h_ref[i] = kb * q / (p_ref[i] + kb * q)
        g_ref[i] = m * q / (n_ref[i] * q + p_ref[i] * m - m * q)
    run = one
    for i in range(depth):
        a_ref[i] = g_ref[i] * run
        run = run * f_ref[i]
    run = one
    for i in reversed(range(depth)):
        b_ref[i] = g_ref[i] * run
        run = run * h_ref[i]
    zero = jnp.zeros(shape, jnp.float32)
    run = one
    for s in reversed(range(groups)):
        below = s < me
        w_ref[s] = jnp.where(below, run, zero)
        run = jnp.where(below, run * up_ref[s], one)
    run = one
    for s in range(groups):
        above = s > me
        w_ref[s] = w_ref[s] + jnp.where(above, run, zero)
        run = jnp.where(above, run * down_ref[s], one)


def coefficients(ax, aw, ay, mask):
    south = pltpu.roll(ay, 1, 1)
    ax_up, ay_up, as_up = jnp.maximum(ax, 0.0), jnp.maximum(ay, 0.0), jnp.maximum(south, 0.0)
    ax_down, ay_down, as_down = jnp.minimum(ax, 0.0), jnp.minimum(ay, 0.0), jnp.minimum(south, 0.0)
    own = (1.0 - 4.0 * DIFFUSION) - ax_up - (ay_up - as_down)
    west = DIFFUSION
    if aw is not None:
        own = own + jnp.minimum(aw, 0.0)
        west = west + jnp.maximum(aw, 0.0)
    return own * mask, (DIFFUSION - ax_down) * mask, west * mask, (DIFFUSION - ay_down) * mask, (DIFFUSION + as_up) * mask


def substep(k_ref, r, own, east, west):
    north = pltpu.roll(own, own.shape[1] - 1, 1)
    south = pltpu.roll(own, 1, 1)
    return (k_ref[0, r] * own + k_ref[1, r] * east) + (k_ref[2, r] * west + k_ref[3, r] * north) + k_ref[4, r] * south


def with_strips(cells, side, row):
    by = (TILE - HSTEPS - 2 * HSTEPS * row) % TILE
    return jnp.concatenate([cells, pltpu.roll(side, by, 1) if by else side], axis=1)


def inside_mask(depth, width, gy, n_gy):
    lane = lax.broadcasted_iota(jnp.int32, (depth, TILE), 1)
    sides = jnp.where((lane < HSTEPS) & (gy < n_gy - 1) | (lane >= TILE - HSTEPS) & (gy > 0), 1.0, 0.0)
    return jnp.concatenate([jnp.ones((depth, width), jnp.float32), sides], axis=1)


def inner_kernel(idx_ref, own_ref, side_lo_ref, side_hi_ref, k_ref, edge_ref, wind_ref, c_ref):
    gy, n_gy = idx_ref[1], idx_ref[4]
    _, rows, depth, width = own_ref.shape
    half = rows // 2
    mask = inside_mask(depth, width, gy, n_gy)

    def plane(a, x):
        side = side_lo_ref[a] if x < half else side_hi_ref[a]
        return with_strips(own_ref[a, x], side, x % half)

    aw = None
    for x in range(rows):
        c_ref[0, x] = plane(0, x)
        ax = plane(1, x)
        for i, k in enumerate(coefficients(ax, aw, plane(2, x), mask)):
            k_ref[i, x] = k
        aw = ax
    wind_ref[...] = aw
    for step in range(HSTEPS):
        src = step % 2
        for i, x in enumerate((step, step + 1, rows - 2 - step, rows - 1 - step)):
            edge_ref[step, i] = c_ref[src, x]
        for x in range(step + 1, rows - 1 - step):
            c_ref[1 - src, x] = substep(k_ref, x, c_ref[src, x], c_ref[src, x + 1], c_ref[src, x - 1])


def outer_kernel(low, idx_ref, got_ref, inner_ref, edge_ref, wind_ref, f_ref, h_ref, g_ref, emission_ref,
                 u_ref, send_ref, c_ref, k_ref, t_ref):
    gx, gy, me = idx_ref[0], idx_ref[1], idx_ref[2]
    n_gx, n_gy = idx_ref[3], idx_ref[4]
    depth, half, width = u_ref.shape
    groups = send_ref.shape[0]
    strip = HSTEPS
    inside = inside_mask(depth, width, gy, n_gy)
    halo_in = inside * jnp.where(gx > 0 if low else gx < n_gx - 1, 1.0, 0.0)
    n_got = 3 * half - (1 if low else 2)

    def plane(a, r):
        side = got_ref[n_got + a // 2, :, pl.ds(a % 2 * TILE, TILE)]
        return with_strips(got_ref[half * a + r - (a == 2)], side, r)

    first = 0 if low else half + 1
    aw = plane(1, 0) if low else wind_ref[...]
    if low:
        c_ref[0, 0] = plane(0, 0)
    else:
        c_ref[0, first + strip - 1] = plane(0, strip - 1)
    for r in range(1, strip) if low else range(strip - 1):
        c_ref[0, first + r] = plane(0, r)
        ax = plane(1, r)
        for i, k in enumerate(coefficients(ax, aw, plane(2, r), halo_in)):
            k_ref[i, r] = k
        aw = ax
    if low:
        for i in range(5):
            k = inner_ref[i, 0]
            if i == 0:
                k = k + jnp.minimum(aw, 0.0) * inside
            if i == 2:
                k = k + jnp.maximum(aw, 0.0) * inside
            k_ref[i, strip] = k

    for step in range(1, strip + 1):
        src = (step - 1) % 2
        reach = strip - 1 + step if low else half + 1 - step

        def at(q):
            if low and q >= reach:
                return edge_ref[step - 1, q - reach]
            if not low and q <= reach:
                return edge_ref[step - 1, q - reach + 3]
            return c_ref[src, q]

        for i in range(strip):
            r = (step if low else reach) + i
            if low:
                weights, row = (k_ref, r) if r <= strip else (inner_ref, r - strip)
            else:
                weights, row = (k_ref, r - first) if r >= first else (inner_ref, r + half - 1)
            new = substep(weights, row, at(r), at(r + 1), at(r - 1))
            if step < strip:
                c_ref[1 - src, r] = new
            else:
                c_ref[1 - src, r, :, :width] = new[:, :width]
    last = strip % 2
    begin = strip if low else 1

    def level(z):
        d = c_ref[last, begin : begin + half, z, :width]
        if z == 0:
            mine = emission_ref[:half] if low else emission_ref[half:]
            d = d + mine * jnp.where(me == 0, 1.0, 0.0)
        return d

    mine = pl.ds(0 if low else half, half)
    run = None
    for z in range(depth):
        d = level(z)
        run = d if z == 0 else d + f_ref[z - 1, mine] * run
        t_ref[z] = run - d
    beta = f_ref[depth - 1, mine] * run
    run = None
    for z in reversed(range(depth)):
        d = level(z)
        run = d if z == depth - 1 else d + h_ref[z + 1, mine] * run
        u_ref[z] = g_ref[z, mine] * (t_ref[z] + run)
    gamma = h_ref[0, mine] * run
    for s in range(groups):
        send_ref[s] = jnp.where(s > me, beta, gamma)


def finish_kernel(idx_ref, west_ref, east_ref, a_ref, b_ref, w_ref, got_ref, out_hbm, out_ref, sems):
    me = idx_ref[2]
    depth, rows, width = a_ref.shape
    groups, half, part = w_ref.shape[0], rows // 2, depth // PARTS
    zero = jnp.zeros((rows, width), jnp.float32)
    below, above = zero, zero
    for s in range(groups):
        term = w_ref[s] * got_ref[s]
        below = below + jnp.where(s < me, term, zero)
        above = above + jnp.where(s > me, term, zero)
    copies = []
    for q in range(PARTS):
        for z in range(q * part, (q + 1) * part):
            more = a_ref[z] * below + b_ref[z] * above
            out_ref[z, :half] = west_ref[z] + more[:half]
            out_ref[z, half:] = east_ref[z] + more[half:]
        at = pl.ds(q * part, part)
        copies.append(pltpu.make_async_copy(out_ref.at[at], out_hbm.at[at], sems.at[q]))
        copies[-1].start()
    for copy in copies:
        copy.wait()


def shifted(x, axis, by):
    length = lax.axis_size(axis)
    return lax.ppermute(x, axis, [(i, i + by) for i in range(length) if 0 <= i + by < length])


def local(conc, wind_x, wind_y, profiles, classes, heights, emission):
    species, depth, rows, width = conc.shape
    groups = lax.axis_size("gz")
    half, wide = rows // 2, width + TILE
    idx = jnp.stack(
        [lax.axis_index("gx"), lax.axis_index("gy"), lax.axis_index("gz"),
         jnp.int32(lax.axis_size("gx")), jnp.int32(lax.axis_size("gy"))]
    ).astype(jnp.int32)
    block, pane, tile, row = (depth, rows, width), (rows, width), (depth, TILE), (depth, wide)
    n_lo, n_hi = 3 * half - 2, 3 * half - 1

    small = (profiles, classes, heights, emission[0])
    own, left, right, profiles, classes, heights, emission = call(
        pack_kernel, [SMEM] + [HBM] * 7,
        [(3, rows, depth, width), (3, *tile), (3, *tile), *(jax.ShapeDtypeStruct(x.shape, x.dtype) for x in small)],
        [(3, *block), pltpu.SemaphoreType.DMA((3 * PARTS,)), pltpu.SemaphoreType.DMA((len(small),))], 1 << 20,
    )(idx, *(pltpu.with_memory_space_constraint(x, pltpu.HBM) for x in (conc[0], wind_x, wind_y, *small)))
    south = shifted(right, "gy", 1)
    north = shifted(left, "gy", -1)
    (k,) = call(table_kernel, [SMEM, VMEM, VMEM], [(depth * groups + 1, *pane)], [], 1 << 24)(
        profiles, classes, heights
    )
    own, south, north, k = lax.optimization_barrier((own, south, north, k))
    lo, hi, side_lo, side_hi = call(
        send_kernel, [VMEM] * 3,
        [(n_lo + 2, depth, width), (n_hi + 2, depth, width), (3, *tile), (3, *tile)], [], 1 << 20
    )(own, south, north)
    west = shifted(hi, "gx", 1)
    east = shifted(lo, "gx", -1)
    weights, edge, wind = call(
        inner_kernel, [SMEM] + [VMEM] * 3,
        [(5, rows, *row), (HSTEPS, 4, *row), row], [(2, rows, *row)], 1 << 24,
    )(idx, own, side_lo, side_hi)
    twice = (2 * depth, rows, width)
    f, h, g, a, b, w = call(
        factor_kernel, [SMEM, VMEM], [block] * 5 + [(groups, *pane)],
        [twice] * 4 + [(groups, *pane)] * 2, 1 << 24,
    )(idx, k)
    halves = []
    for low, got in ((True, west), (False, east)):
        if not low:
            wind, _ = lax.optimization_barrier((wind, halves[0][1]))
        halves.append(call(
            functools.partial(outer_kernel, low), [SMEM] + [VMEM] * 8,
            [(depth, half, width), (groups, half, width)],
            [(2, half + HSTEPS + 1, *row), (5, HSTEPS + 1, *row), (depth, half, width)], 1 << 24,
        )(idx, got, weights, edge, wind, f, h, g, emission))
    send = jnp.concatenate([s for _, s in halves], axis=1)
    got = lax.all_to_all(send, "gz", split_axis=0, concat_axis=0, tiled=True)
    (out,) = call(
        finish_kernel, [SMEM] + [VMEM] * 6, [block], [block, pltpu.SemaphoreType.DMA((PARTS,))], 1 << 20, HBM
    )(idx, *(u for u, _ in halves), a, b, w, got)
    return out[None]


def solution(mesh):
    return jax.shard_map(
        local,
        mesh=mesh,
        in_specs=(
            P(None, "gz", "gx", "gy"),
            P("gz", "gx", "gy"),
            P("gz", "gx", "gy"),
            P(),
            P("gx", "gy"),
            P("gx", "gy"),
            P(None, "gx", "gy"),
        ),
        out_specs=P(None, "gz", "gx", "gy"),
        check_vma=False,
    )
```

```python
import functools

import jax
import jax.numpy as jnp
from jax import lax
from jax.experimental import pallas as pl
from jax.experimental.pallas import tpu as pltpu
from jax.sharding import PartitionSpec as P

HSTEPS = 8
NCLASS = 8
TILE = 128
DIFFUSION = 0.05
CANOPY = 0.2
LIMIT = 8 * 1024 * 1024
PARTS = 4
LEVELS = 8

VMEM = pl.BlockSpec(memory_space=pltpu.VMEM)
SMEM = pl.BlockSpec(memory_space=pltpu.SMEM)
HBM = pl.BlockSpec(memory_space=pltpu.HBM)


def call(kernel, ins, outs, scratch, flops):
    return pl.pallas_call(
        kernel,
        out_shape=[jax.ShapeDtypeStruct(s, jnp.float32) if isinstance(s, tuple) else s for s in outs],
        in_specs=ins,
        out_specs=[VMEM] * len(outs),
        scratch_shapes=[pltpu.VMEM(s, jnp.float32) if isinstance(s, tuple) else s for s in scratch],
        compiler_params=pltpu.CompilerParams(vmem_limit_bytes=LIMIT),
        cost_estimate=pl.CostEstimate(flops=flops, bytes_accessed=1 << 20, transcendentals=0),
    )


def pack_kernel(idx_ref, c_hbm, wx_hbm, wy_hbm, *refs):
    small, (own_ref, yl_ref, yr_ref), kept, (in_ref, sems, small_sems) = refs[:4], refs[4:7], refs[7:11], refs[11:]
    depth, rows, width = c_hbm.shape
    half, strip, part = rows // 2, HSTEPS, depth // PARTS
    copies = []
    for a, ref in enumerate((c_hbm, wx_hbm, wy_hbm)):
        for q in range(PARTS):
            at = pl.ds(q * part, part)
            copies.append(pltpu.make_async_copy(ref.at[at], in_ref.at[a, at], sems.at[a * PARTS + q]))
            copies[-1].start()
    others = [pltpu.make_async_copy(s, d, small_sems.at[i]) for i, (s, d) in enumerate(zip(small, kept))]
    for copy in others:
        copy.start()
    lane = lax.broadcasted_iota(jnp.int32, (depth, TILE), 1) // strip
    for a in range(3):
        for q in range(PARTS):
            copies[a * PARTS + q].wait()
        left = jnp.zeros((depth, TILE), jnp.float32)
        right = left
        for x in range(rows):
            row = in_ref[a, :, x, :]
            own_ref[a, x] = row
            first, last = row[:, :TILE], row[:, width - TILE :]
            group = 2 * (x % half)
            to_left, to_right = group + 1 - x // half, group + x // half
            if to_left:
                first = pltpu.roll(first, strip * to_left, 1)
            if (to_right + 1) * strip % TILE:
                last = pltpu.roll(last, (to_right + 1) * strip % TILE, 1)
            left = jnp.where(lane == to_left, first, left)
            right = jnp.where(lane == to_right, last, right)
        yl_ref[a] = left
        yr_ref[a] = right
    for copy in others:
        copy.wait()


def send_kernel(own_ref, south_ref, north_ref, lo_ref, hi_ref, side_lo_ref, side_hi_ref):
    _, rows, depth, width = own_ref.shape
    half = rows // 2
    to_lo, to_hi = 0, 0
    for a in range(3):
        for x in range(rows):
            first, last = own_ref[a, x, :, :TILE], own_ref[a, x, :, TILE:]
            if x < half and not (a > 0 and x == half - 1):
                lo_ref[to_lo], lo_ref[to_lo + 1] = first, last
                to_lo += 2
            if x >= half and not (a == 2 and x == half):
                hi_ref[to_hi], hi_ref[to_hi + 1] = first, last
                to_hi += 2
    even = lax.broadcasted_iota(jnp.int32, (depth, TILE), 1) // HSTEPS % 2 == 0
    for a in range(3):
        south, north = south_ref[a], north_ref[a]
        low = jnp.where(even, south, north)
        high = jnp.where(even, pltpu.roll(south, TILE - HSTEPS, 1), pltpu.roll(north, HSTEPS, 1))
        side_lo_ref[a] = low
        side_hi_ref[a] = high
        lo_ref[to_lo + a] = low
        hi_ref[to_hi + a] = high


def mixing_numbers(profiles_ref, classes_ref, heights_ref, k_ref):
    total = k_ref.shape[0] - 1
    classes, heights = classes_ref[...], heights_ref[...]
    bits = [(classes & (1 << b)) != 0 for b in range(3)]
    k_ref[0] = jnp.zeros(classes.shape, jnp.float32)

    def mixing(z, _):
        table = [profiles_ref[c, z] for c in range(NCLASS)]
        for bit in bits:
            table = [jnp.where(bit, table[i + 1], table[i]) for i in range(0, len(table), 2)]
        k = table[0]
        k_ref[z + 1] = jnp.where(z < heights, CANOPY * k, k)
        return 0

    lax.fori_loop(0, total, mixing, 0, unroll=8)


def factor_kernel(idx_ref, profiles_ref, classes_ref, heights_ref, f_ref, h_ref, g_ref, a_ref, b_ref, w_ref,
                  k_ref, n_ref, m_ref, p_ref, q_ref, up_ref, down_ref):
    me = idx_ref[2]
    depth = g_ref.shape[0]
    groups = w_ref.shape[0]
    shape = w_ref.shape[1:]
    total = depth * groups
    one = jnp.ones(shape, jnp.float32)
    mixing_numbers(profiles_ref, classes_ref, heights_ref, k_ref)

    def some(t, carry):
        n, p, up, down = carry
        low = t * LEVELS
        high = total - 1 - low
        chunk_n, chunk_p = low // depth, high // depth
        at_n = low % depth + jnp.where(chunk_n == me, 0, depth)
        at_p = high % depth + jnp.where(chunk_p == me, 0, depth)
        m, q = one, one
        for i in range(LEVELS):
            k, kb = k_ref[low + i + 1], k_ref[high - i]
            n_ref[at_n + i], m_ref[at_n + i] = n, m
            p_ref[at_p - i], q_ref[at_p - i] = p, q
            m, q = n + k * m, p + kb * q
            n, p = m + k * n, q + kb * p
            up, down = up * k, down * kb
        m, q = 1.0 / m, 1.0 / q
        up, down = up * m, down * q
        up_ref[chunk_n], down_ref[chunk_p] = up, down
        fresh = low % depth + LEVELS == depth
        return n * m, p * q, jnp.where(fresh, one, up), jnp.where(fresh, one, down)

    lax.fori_loop(0, total // LEVELS, some, (one, 1.0 + k_ref[total], one, one))

    begin = me * depth
    for i in range(depth):
        m, q = m_ref[i], q_ref[i]
        k, kb = k_ref[begin + i + 1], k_ref[begin + i]
        f_ref[i] = k * m / (n_ref[i] + k * m)
        h_ref[i] = kb * q / (p_ref[i] + kb * q)
        g_ref[i] = m * q / (n_ref[i] * q + p_ref[i] * m - m * q)
    run = one
    for i in range(depth):
        a_ref[i] = g_ref[i] * run
        run = run * f_ref[i]
    run = one
    for i in reversed(range(depth)):
        b_ref[i] = g_ref[i] * run
        run = run * h_ref[i]
    zero = jnp.zeros(shape, jnp.float32)
    run = one
    for s in reversed(range(groups)):
        below = s < me
        w_ref[s] = jnp.where(below, run, zero)
        run = jnp.where(below, run * up_ref[s], one)
    run = one
    for s in range(groups):
        above = s > me
        w_ref[s] = w_ref[s] + jnp.where(above, run, zero)
        run = jnp.where(above, run * down_ref[s], one)


def coefficients(ax, aw, ay, mask):
    south = pltpu.roll(ay, 1, 1)
    ax_up, ay_up, as_up = jnp.maximum(ax, 0.0), jnp.maximum(ay, 0.0), jnp.maximum(south, 0.0)
    ax_down, ay_down, as_down = jnp.minimum(ax, 0.0), jnp.minimum(ay, 0.0), jnp.minimum(south, 0.0)
    own = (1.0 - 4.0 * DIFFUSION) - ax_up - (ay_up - as_down)
    west = DIFFUSION
    if aw is not None:
        own = own + jnp.minimum(aw, 0.0)
        west = west + jnp.maximum(aw, 0.0)
    return own * mask, (DIFFUSION - ax_down) * mask, west * mask, (DIFFUSION - ay_down) * mask, (DIFFUSION + as_up) * mask


def substep(k_ref, r, own, east, west):
    north = pltpu.roll(own, own.shape[1] - 1, 1)
    south = pltpu.roll(own, 1, 1)
    return (k_ref[0, r] * own + k_ref[1, r] * east) + (k_ref[2, r] * west + k_ref[3, r] * north) + k_ref[4, r] * south


def with_strips(first, last, side, row):
    by = (TILE - HSTEPS - 2 * HSTEPS * row) % TILE
    return jnp.concatenate([first, last, pltpu.roll(side, by, 1) if by else side], axis=1)


def inside_mask(depth, width, gy, n_gy):
    lane = lax.broadcasted_iota(jnp.int32, (depth, TILE), 1)
    sides = jnp.where((lane < HSTEPS) & (gy < n_gy - 1) | (lane >= TILE - HSTEPS) & (gy > 0), 1.0, 0.0)
    return jnp.concatenate([jnp.ones((depth, width), jnp.float32), sides], axis=1)


def inner_kernel(idx_ref, own_ref, side_lo_ref, side_hi_ref, k_ref, edge_ref, wind_ref, c_ref):
    gy, n_gy = idx_ref[1], idx_ref[4]
    _, rows, depth, width = own_ref.shape
    half = rows // 2
    mask = inside_mask(depth, width, gy, n_gy)

    def plane(a, x):
        side = side_lo_ref[a] if x < half else side_hi_ref[a]
        return with_strips(own_ref[a, x, :, :TILE], own_ref[a, x, :, TILE:], side, x % half)

    aw = None
    for x in range(rows):
        c_ref[0, x] = plane(0, x)
        ax = plane(1, x)
        for i, k in enumerate(coefficients(ax, aw, plane(2, x), mask)):
            k_ref[i, x] = k
        aw = ax
    wind_ref[...] = aw
    for step in range(HSTEPS):
        src = step % 2
        for i, x in enumerate((step, step + 1, rows - 2 - step, rows - 1 - step)):
            edge_ref[step, i] = c_ref[src, x]
        for x in range(step + 1, rows - 1 - step):
            c_ref[1 - src, x] = substep(k_ref, x, c_ref[src, x], c_ref[src, x + 1], c_ref[src, x - 1])


def outer_kernel(low, idx_ref, got_ref, inner_ref, edge_ref, wind_ref, f_ref, h_ref, g_ref, emission_ref,
                 u_ref, send_ref, c_ref, k_ref, t_ref):
    gx, gy, me = idx_ref[0], idx_ref[1], idx_ref[2]
    n_gx, n_gy = idx_ref[3], idx_ref[4]
    depth, half, width = u_ref.shape
    groups = send_ref.shape[0]
    strip = HSTEPS
    inside = inside_mask(depth, width, gy, n_gy)
    halo_in = inside * jnp.where(gx > 0 if low else gx < n_gx - 1, 1.0, 0.0)
    n_got = 6 * half - (2 if low else 4)

    def plane(a, r):
        at = 2 * (half * a + r - (a == 2))
        return with_strips(got_ref[at], got_ref[at + 1], got_ref[n_got + a], r)

    first = 0 if low else half + 1
    aw = plane(1, 0) if low else wind_ref[...]
    if low:
        c_ref[0, 0] = plane(0, 0)
    else:
        c_ref[0, first + strip - 1] = plane(0, strip - 1)
    for r in range(1, strip) if low else range(strip - 1):
        c_ref[0, first + r] = plane(0, r)
        ax = plane(1, r)
        for i, k in enumerate(coefficients(ax, aw, plane(2, r), halo_in)):
            k_ref[i, r] = k
        aw = ax
    if low:
        for i in range(5):
            k = inner_ref[i, 0]
            if i == 0:
                k = k + jnp.minimum(aw, 0.0) * inside
            if i == 2:
                k = k + jnp.maximum(aw, 0.0) * inside
            k_ref[i, strip] = k

    for step in range(1, strip + 1):
        src = (step - 1) % 2
        reach = strip - 1 + step if low else half + 1 - step

        def at(q):
            if low and q >= reach:
                return edge_ref[step - 1, q - reach]
            if not low and q <= reach:
                return edge_ref[step - 1, q - reach + 3]
            return c_ref[src, q]

        for i in range(strip):
            r = (step if low else reach) + i
            if low:
                weights, row = (k_ref, r) if r <= strip else (inner_ref, r - strip)
            else:
                weights, row = (k_ref, r - first) if r >= first else (inner_ref, r + half - 1)
            new = substep(weights, row, at(r), at(r + 1), at(r - 1))
            if step < strip:
                c_ref[1 - src, r] = new
            else:
                c_ref[1 - src, r, :, :width] = new[:, :width]
    last = strip % 2
    begin = strip if low else 1

    def level(z):
        d = c_ref[last, begin : begin + half, z, :width]
        if z == 0:
            mine = emission_ref[:half] if low else emission_ref[half:]
            d = d + mine * jnp.where(me == 0, 1.0, 0.0)
        return d

    mine = pl.ds(0 if low else half, half)
    run = None
    for z in range(depth):
        d = level(z)
        run = d if z == 0 else d + f_ref[z - 1, mine] * run
        t_ref[z] = run - d
    beta = f_ref[depth - 1, mine] * run
    run = None
    for z in reversed(range(depth)):
        d = level(z)
        run = d if z == depth - 1 else d + h_ref[z + 1, mine] * run
        u_ref[z] = g_ref[z, mine] * (t_ref[z] + run)
    gamma = h_ref[0, mine] * run
    for s in range(groups):
        send_ref[s] = jnp.where(s > me, beta, gamma)


def finish_kernel(idx_ref, west_ref, east_ref, a_ref, b_ref, w_ref, got_ref, out_ref):
    me = idx_ref[2]
    depth, rows, width = a_ref.shape
    groups, half = w_ref.shape[0], rows // 2
    zero = jnp.zeros((rows, width), jnp.float32)
    below, above = zero, zero
    for s in range(groups):
        term = w_ref[s] * got_ref[s]
        below = below + jnp.where(s < me, term, zero)
        above = above + jnp.where(s > me, term, zero)
    for z in range(depth):
        more = a_ref[z] * below + b_ref[z] * above
        out_ref[z, :half] = west_ref[z] + more[:half]
        out_ref[z, half:] = east_ref[z] + more[half:]


def shifted(x, axis, by):
    length = lax.axis_size(axis)
    return lax.ppermute(x, axis, [(i, i + by) for i in range(length) if 0 <= i + by < length])


def local(conc, wind_x, wind_y, profiles, classes, heights, emission):
    species, depth, rows, width = conc.shape
    groups = lax.axis_size("gz")
    half, wide = rows // 2, width + TILE
    idx = jnp.stack(
        [lax.axis_index("gx"), lax.axis_index("gy"), lax.axis_index("gz"),
         jnp.int32(lax.axis_size("gx")), jnp.int32(lax.axis_size("gy"))]
    ).astype(jnp.int32)
    block, pane, tile, row = (depth, rows, width), (rows, width), (depth, TILE), (depth, wide)
    n_lo, n_hi = 6 * half - 4, 6 * half - 2

    small = (profiles, classes, heights, emission[0])
    own, left, right, profiles, classes, heights, emission = call(
        pack_kernel, [SMEM] + [HBM] * 7,
        [(3, rows, depth, width), (3, *tile), (3, *tile), *(jax.ShapeDtypeStruct(x.shape, x.dtype) for x in small)],
        [(3, *block), pltpu.SemaphoreType.DMA((3 * PARTS,)), pltpu.SemaphoreType.DMA((len(small),))], 1 << 20,
    )(idx, *(pltpu.with_memory_space_constraint(x, pltpu.HBM) for x in (conc[0], wind_x, wind_y, *small)))
    south = shifted(right, "gy", 1)
    north = shifted(left, "gy", -1)
    lo, hi, side_lo, side_hi = call(
        send_kernel, [VMEM] * 3,
        [(n_lo + 3, *tile), (n_hi + 3, *tile), (3, *tile), (3, *tile)], [], 1 << 20
    )(own, south, north)
    west = shifted(hi, "gx", 1)
    east = shifted(lo, "gx", -1)
    weights, edge, wind = call(
        inner_kernel, [SMEM] + [VMEM] * 3,
        [(5, rows, *row), (HSTEPS, 4, *row), row], [(2, rows, *row)], 1 << 24,
    )(idx, own, side_lo, side_hi)
    twice = (2 * depth, rows, width)
    profiles, _ = lax.optimization_barrier((profiles, side_lo))
    f, h, g, a, b, w = call(
        factor_kernel, [SMEM, SMEM, VMEM, VMEM], [block] * 5 + [(groups, *pane)],
        [(depth * groups + 1, *pane)] + [twice] * 4 + [(groups, *pane)] * 2, 1 << 24,
    )(idx, profiles, classes, heights)
    halves = []
    for low, got in ((True, west), (False, east)):
        if not low:
            wind, _ = lax.optimization_barrier((wind, halves[0][1]))
        halves.append(call(
            functools.partial(outer_kernel, low), [SMEM] + [VMEM] * 8,
            [(depth, half, width), (groups, half, width)],
            [(2, half + HSTEPS + 1, *row), (5, HSTEPS + 1, *row), (depth, half, width)], 1 << 24,
        )(idx, got, weights, edge, wind, f, h, g, emission))
    send = jnp.concatenate([s for _, s in halves], axis=1)
    got = lax.all_to_all(send, "gz", split_axis=0, concat_axis=0, tiled=True)
    (out,) = call(
        finish_kernel, [SMEM] + [VMEM] * 6, [block], [], 1 << 20
    )(idx, *(u for u, _ in halves), a, b, w, got)
    return out[None]


def solution(mesh):
    return jax.shard_map(
        local,
        mesh=mesh,
        in_specs=(
            P(None, "gz", "gx", "gy"),
            P("gz", "gx", "gy"),
            P("gz", "gx", "gy"),
            P(),
            P("gx", "gy"),
            P("gx", "gy"),
            P(None, "gx", "gy"),
        ),
        out_specs=P(None, "gz", "gx", "gy"),
        check_vma=False,
    )
```

```python
import functools

import jax
import jax.numpy as jnp
from jax import lax
from jax.experimental import pallas as pl
from jax.experimental.pallas import tpu as pltpu
from jax.sharding import PartitionSpec as P

HSTEPS = 8
NCLASS = 8
TILE = 128
DIFFUSION = 0.05
CANOPY = 0.2
LIMIT = 8 * 1024 * 1024
PARTS = 4
LEVELS = 8

VMEM = pl.BlockSpec(memory_space=pltpu.VMEM)
SMEM = pl.BlockSpec(memory_space=pltpu.SMEM)
HBM = pl.BlockSpec(memory_space=pltpu.HBM)


def call(kernel, ins, outs, scratch, flops):
    return pl.pallas_call(
        kernel,
        out_shape=[jax.ShapeDtypeStruct(s, jnp.float32) if isinstance(s, tuple) else s for s in outs],
        in_specs=ins,
        out_specs=[VMEM] * len(outs),
        scratch_shapes=[pltpu.VMEM(s, jnp.float32) if isinstance(s, tuple) else s for s in scratch],
        compiler_params=pltpu.CompilerParams(vmem_limit_bytes=LIMIT),
        cost_estimate=pl.CostEstimate(flops=flops, bytes_accessed=1 << 20, transcendentals=0),
    )


def pack_kernel(c_hbm, wx_hbm, wy_hbm, *refs):
    small, (own_ref, yl_ref, yr_ref), kept, (in_ref, sems, small_sems) = refs[:4], refs[4:7], refs[7:11], refs[11:]
    depth, rows, width = c_hbm.shape
    half, strip, part = rows // 2, HSTEPS, depth // PARTS
    copies = []
    for a, ref in enumerate((c_hbm, wx_hbm, wy_hbm)):
        for q in range(PARTS):
            at = pl.ds(q * part, part)
            copies.append(pltpu.make_async_copy(ref.at[at], in_ref.at[a, at], sems.at[a * PARTS + q]))
            copies[-1].start()
    others = [pltpu.make_async_copy(s, d, small_sems.at[i]) for i, (s, d) in enumerate(zip(small, kept))]
    for copy in others:
        copy.start()
    lane = lax.broadcasted_iota(jnp.int32, (depth, TILE), 1) // strip
    for a in range(3):
        for q in range(PARTS):
            copies[a * PARTS + q].wait()
        left = jnp.zeros((depth, TILE), jnp.float32)
        right = left
        for x in range(rows):
            row = in_ref[a, :, x, :]
            own_ref[a, x] = row
            first, last = row[:, :TILE], row[:, width - TILE :]
            group = 2 * (x % half)
            to_left, to_right = group + 1 - x // half, group + x // half
            if to_left:
                first = pltpu.roll(first, strip * to_left, 1)
            if (to_right + 1) * strip % TILE:
                last = pltpu.roll(last, (to_right + 1) * strip % TILE, 1)
            left = jnp.where(lane == to_left, first, left)
            right = jnp.where(lane == to_right, last, right)
        yl_ref[a] = left
        yr_ref[a] = right
    for copy in others:
        copy.wait()


def send_kernel(own_ref, south_ref, north_ref, lo_ref, hi_ref, side_lo_ref, side_hi_ref):
    _, rows, depth, width = own_ref.shape
    half = rows // 2
    to_lo, to_hi = 0, 0
    for a in range(3):
        for x in range(rows):
            first, last = own_ref[a, x, :, :TILE], own_ref[a, x, :, TILE:]
            if x < half and not (a > 0 and x == half - 1):
                lo_ref[to_lo], lo_ref[to_lo + 1] = first, last
                to_lo += 2
            if x >= half and not (a == 2 and x == half):
                hi_ref[to_hi], hi_ref[to_hi + 1] = first, last
                to_hi += 2
    even = lax.broadcasted_iota(jnp.int32, (depth, TILE), 1) // HSTEPS % 2 == 0
    for a in range(3):
        south, north = south_ref[a], north_ref[a]
        low = jnp.where(even, south, north)
        high = jnp.where(even, pltpu.roll(south, TILE - HSTEPS, 1), pltpu.roll(north, HSTEPS, 1))
        side_lo_ref[a] = low
        side_hi_ref[a] = high
        lo_ref[to_lo + a] = low
        hi_ref[to_hi + a] = high


def mixing_numbers(profiles_ref, classes_ref, heights_ref, k_ref):
    total = k_ref.shape[0] - 1
    classes, heights = classes_ref[...], heights_ref[...]
    bits = [(classes & (1 << b)) != 0 for b in range(3)]
    k_ref[0] = jnp.zeros(classes.shape, jnp.float32)

    def mixing(z, _):
        table = [profiles_ref[c, z] for c in range(NCLASS)]
        for bit in bits:
            table = [jnp.where(bit, table[i + 1], table[i]) for i in range(0, len(table), 2)]
        k = table[0]
        k_ref[z + 1] = jnp.where(z < heights, CANOPY * k, k)
        return 0

    lax.fori_loop(0, total, mixing, 0, unroll=8)


def factor_kernel(profiles_ref, classes_ref, heights_ref, f_ref, h_ref, g_ref, a_ref, b_ref, w_ref,
                  k_ref, n_ref, m_ref, p_ref, q_ref, up_ref, down_ref):
    me = lax.axis_index("gz")
    depth = g_ref.shape[0]
    groups = w_ref.shape[0]
    shape = w_ref.shape[1:]
    total = depth * groups
    one = jnp.ones(shape, jnp.float32)
    mixing_numbers(profiles_ref, classes_ref, heights_ref, k_ref)

    def some(t, carry):
        n, p, up, down = carry
        low = t * LEVELS
        high = total - 1 - low
        chunk_n, chunk_p = low // depth, high // depth
        at_n = low % depth + jnp.where(chunk_n == me, 0, depth)
        at_p = high % depth + jnp.where(chunk_p == me, 0, depth)
        m, q = one, one
        for i in range(LEVELS):
            k, kb = k_ref[low + i + 1], k_ref[high - i]
            n_ref[at_n + i], m_ref[at_n + i] = n, m
            p_ref[at_p - i], q_ref[at_p - i] = p, q
            m, q = n + k * m, p + kb * q
            n, p = m + k * n, q + kb * p
            up, down = up * k, down * kb
        m, q = 1.0 / m, 1.0 / q
        up, down = up * m, down * q
        up_ref[chunk_n], down_ref[chunk_p] = up, down
        fresh = low % depth + LEVELS == depth
        return n * m, p * q, jnp.where(fresh, one, up), jnp.where(fresh, one, down)

    lax.fori_loop(0, total // LEVELS, some, (one, 1.0 + k_ref[total], one, one))

    begin = me * depth
    for i in range(depth):
        m, q = m_ref[i], q_ref[i]
        k, kb = k_ref[begin + i + 1], k_ref[begin + i]
        f_ref[i] = k * m / (n_ref[i] + k * m)
        h_ref[i] = kb * q / (p_ref[i] + kb * q)
        g_ref[i] = m * q / (n_ref[i] * q + p_ref[i] * m - m * q)
    run = one
    for i in range(depth):
        a_ref[i] = g_ref[i] * run
        run = run * f_ref[i]
    run = one
    for i in reversed(range(depth)):
        b_ref[i] = g_ref[i] * run
        run = run * h_ref[i]
    zero = jnp.zeros(shape, jnp.float32)
    run = one
    for s in reversed(range(groups)):
        below = s < me
        w_ref[s] = jnp.where(below, run, zero)
        run = jnp.where(below, run * up_ref[s], one)
    run = one
    for s in range(groups):
        above = s > me
        w_ref[s] = w_ref[s] + jnp.where(above, run, zero)
        run = jnp.where(above, run * down_ref[s], one)


def coefficients(ax, aw, ay, mask):
    south = pltpu.roll(ay, 1, 1)
    ax_up, ay_up, as_up = jnp.maximum(ax, 0.0), jnp.maximum(ay, 0.0), jnp.maximum(south, 0.0)
    ax_down, ay_down, as_down = jnp.minimum(ax, 0.0), jnp.minimum(ay, 0.0), jnp.minimum(south, 0.0)
    own = (1.0 - 4.0 * DIFFUSION) - ax_up - (ay_up - as_down)
    west = DIFFUSION
    if aw is not None:
        own = own + jnp.minimum(aw, 0.0)
        west = west + jnp.maximum(aw, 0.0)
    return own * mask, (DIFFUSION - ax_down) * mask, west * mask, (DIFFUSION - ay_down) * mask, (DIFFUSION + as_up) * mask


def substep(k_ref, r, own, east, west):
    north = pltpu.roll(own, own.shape[1] - 1, 1)
    south = pltpu.roll(own, 1, 1)
    return (k_ref[0, r] * own + k_ref[1, r] * east) + (k_ref[2, r] * west + k_ref[3, r] * north) + k_ref[4, r] * south


def with_strips(first, last, side, row):
    by = (TILE - HSTEPS - 2 * HSTEPS * row) % TILE
    return jnp.concatenate([first, last, pltpu.roll(side, by, 1) if by else side], axis=1)


def inside_mask(depth, width):
    gy, n_gy = lax.axis_index("gy"), lax.axis_size("gy")
    lane = lax.broadcasted_iota(jnp.int32, (depth, TILE), 1)
    sides = jnp.where((lane < HSTEPS) & (gy < n_gy - 1) | (lane >= TILE - HSTEPS) & (gy > 0), 1.0, 0.0)
    return jnp.concatenate([jnp.ones((depth, width), jnp.float32), sides], axis=1)


def inner_kernel(own_ref, side_lo_ref, side_hi_ref, k_ref, edge_ref, wind_ref, c_ref):
    _, rows, depth, width = own_ref.shape
    half = rows // 2
    mask = inside_mask(depth, width)

    def plane(a, x):
        side = side_lo_ref[a] if x < half else side_hi_ref[a]
        return with_strips(own_ref[a, x, :, :TILE], own_ref[a, x, :, TILE:], side, x % half)

    aw = None
    for x in range(rows):
        c_ref[0, x] = plane(0, x)
        ax = plane(1, x)
        for i, k in enumerate(coefficients(ax, aw, plane(2, x), mask)):
            k_ref[i, x] = k
        aw = ax
    wind_ref[...] = aw
    for step in range(HSTEPS):
        src = step % 2
        for i, x in enumerate((step, step + 1, rows - 2 - step, rows - 1 - step)):
            edge_ref[step, i] = c_ref[src, x]
        for x in range(step + 1, rows - 1 - step):
            c_ref[1 - src, x] = substep(k_ref, x, c_ref[src, x], c_ref[src, x + 1], c_ref[src, x - 1])


def outer_kernel(low, got_ref, inner_ref, edge_ref, wind_ref, f_ref, h_ref, g_ref, emission_ref,
                 u_ref, send_ref, c_ref, k_ref, t_ref):
    gx, me, n_gx = lax.axis_index("gx"), lax.axis_index("gz"), lax.axis_size("gx")
    depth, half, width = u_ref.shape
    groups = send_ref.shape[0]
    strip = HSTEPS
    inside = inside_mask(depth, width)
    halo_in = inside * jnp.where(gx > 0 if low else gx < n_gx - 1, 1.0, 0.0)
    n_got = 6 * half - (2 if low else 4)

    def plane(a, r):
        at = 2 * (half * a + r - (a == 2))
        return with_strips(got_ref[at], got_ref[at + 1], got_ref[n_got + a], r)

    first = 0 if low else half + 1
    aw = plane(1, 0) if low else wind_ref[...]
    if low:
        c_ref[0, 0] = plane(0, 0)
    else:
        c_ref[0, first + strip - 1] = plane(0, strip - 1)
    for r in range(1, strip) if low else range(strip - 1):
        c_ref[0, first + r] = plane(0, r)
        ax = plane(1, r)
        for i, k in enumerate(coefficients(ax, aw, plane(2, r), halo_in)):
            k_ref[i, r] = k
        aw = ax
    if low:
        for i in range(5):
            k = inner_ref[i, 0]
            if i == 0:
                k = k + jnp.minimum(aw, 0.0) * inside
            if i == 2:
                k = k + jnp.maximum(aw, 0.0) * inside
            k_ref[i, strip] = k

    for step in range(1, strip + 1):
        src = (step - 1) % 2
        reach = strip - 1 + step if low else half + 1 - step

        def at(q):
            if low and q >= reach:
                return edge_ref[step - 1, q - reach]
            if not low and q <= reach:
                return edge_ref[step - 1, q - reach + 3]
            return c_ref[src, q]

        for i in range(strip):
            r = (step if low else reach) + i
            if low:
                weights, row = (k_ref, r) if r <= strip else (inner_ref, r - strip)
            else:
                weights, row = (k_ref, r - first) if r >= first else (inner_ref, r + half - 1)
            new = substep(weights, row, at(r), at(r + 1), at(r - 1))
            if step < strip:
                c_ref[1 - src, r] = new
            else:
                c_ref[1 - src, r, :, :width] = new[:, :width]
    last = strip % 2
    begin = strip if low else 1

    def level(z):
        d = c_ref[last, begin : begin + half, z, :width]
        if z == 0:
            mine = emission_ref[:half] if low else emission_ref[half:]
            d = d + mine * jnp.where(me == 0, 1.0, 0.0)
        return d

    mine = pl.ds(0 if low else half, half)
    run = None
    for z in range(depth):
        d = level(z)
        run = d if z == 0 else d + f_ref[z - 1, mine] * run
        t_ref[z] = run - d
    beta = f_ref[depth - 1, mine] * run
    run = None
    for z in reversed(range(depth)):
        d = level(z)
        run = d if z == depth - 1 else d + h_ref[z + 1, mine] * run
        u_ref[z] = g_ref[z, mine] * (t_ref[z] + run)
    gamma = h_ref[0, mine] * run
    for s in range(groups):
        send_ref[s] = jnp.where(s > me, beta, gamma)


def finish_kernel(west_ref, east_ref, a_ref, b_ref, w_ref, got_ref, out_ref):
    me = lax.axis_index("gz")
    depth, rows, width = a_ref.shape
    groups, half = w_ref.shape[0], rows // 2
    zero = jnp.zeros((rows, width), jnp.float32)
    below, above = zero, zero
    for s in range(groups):
        term = w_ref[s] * got_ref[s]
        below = below + jnp.where(s < me, term, zero)
        above = above + jnp.where(s > me, term, zero)
    for z in range(depth):
        more = a_ref[z] * below + b_ref[z] * above
        out_ref[z, :half] = west_ref[z] + more[:half]
        out_ref[z, half:] = east_ref[z] + more[half:]


def shifted(x, axis, by):
    length = lax.axis_size(axis)
    return lax.ppermute(x, axis, [(i, i + by) for i in range(length) if 0 <= i + by < length])


def local(conc, wind_x, wind_y, profiles, classes, heights, emission):
    species, depth, rows, width = conc.shape
    groups = lax.axis_size("gz")
    half, wide = rows // 2, width + TILE
    block, pane, tile, row = (depth, rows, width), (rows, width), (depth, TILE), (depth, wide)
    n_lo, n_hi = 6 * half - 4, 6 * half - 2

    small = (profiles, classes, heights, emission[0])
    own, left, right, profiles, classes, heights, emission = call(
        pack_kernel, [HBM] * 7,
        [(3, rows, depth, width), (3, *tile), (3, *tile), *(jax.ShapeDtypeStruct(x.shape, x.dtype) for x in small)],
        [(3, *block), pltpu.SemaphoreType.DMA((3 * PARTS,)), pltpu.SemaphoreType.DMA((len(small),))], 1 << 20,
    )(*(pltpu.with_memory_space_constraint(x, pltpu.HBM) for x in (conc[0], wind_x, wind_y, *small)))
    south = shifted(right, "gy", 1)
    north = shifted(left, "gy", -1)
    lo, hi, side_lo, side_hi = call(
        send_kernel, [VMEM] * 3,
        [(n_lo + 3, *tile), (n_hi + 3, *tile), (3, *tile), (3, *tile)], [], 1 << 20
    )(own, south, north)
    west = shifted(hi, "gx", 1)
    east = shifted(lo, "gx", -1)
    weights, edge, wind = call(
        inner_kernel, [VMEM] * 3,
        [(5, rows, *row), (HSTEPS, 4, *row), row], [(2, rows, *row)], 1 << 24,
    )(own, side_lo, side_hi)
    twice = (2 * depth, rows, width)
    profiles, _ = lax.optimization_barrier((profiles, side_lo))
    f, h, g, a, b, w = call(
        factor_kernel, [SMEM, VMEM, VMEM], [block] * 5 + [(groups, *pane)],
        [(depth * groups + 1, *pane)] + [twice] * 4 + [(groups, *pane)] * 2, 1 << 24,
    )(profiles, classes, heights)
    halves = []
    for low, got in ((True, west), (False, east)):
        if not low:
            wind, _ = lax.optimization_barrier((wind, halves[0][1]))
        halves.append(call(
            functools.partial(outer_kernel, low), [VMEM] * 8,
            [(depth, half, width), (groups, half, width)],
            [(2, half + HSTEPS + 1, *row), (5, HSTEPS + 1, *row), (depth, half, width)], 1 << 24,
        )(got, weights, edge, wind, f, h, g, emission))
    send = jnp.concatenate([s for _, s in halves], axis=1)
    got = lax.all_to_all(send, "gz", split_axis=0, concat_axis=0, tiled=True)
    (out,) = call(
        finish_kernel, [VMEM] * 6, [block], [], 1 << 20
    )(*(u for u, _ in halves), a, b, w, got)
    return out[None]


def solution(mesh):
    return jax.shard_map(
        local,
        mesh=mesh,
        in_specs=(
            P(None, "gz", "gx", "gy"),
            P("gz", "gx", "gy"),
            P("gz", "gx", "gy"),
            P(),
            P("gx", "gy"),
            P("gx", "gy"),
            P(None, "gx", "gy"),
        ),
        out_specs=P(None, "gz", "gx", "gy"),
        check_vma=False,
    )
```

```python
import functools

import jax
import jax.numpy as jnp
from jax import lax
from jax.experimental import pallas as pl
from jax.experimental.pallas import tpu as pltpu
from jax.sharding import PartitionSpec as P

HSTEPS = 8
NCLASS = 8
TILE = 128
DIFFUSION = 0.05
CANOPY = 0.2
LIMIT = 8 * 1024 * 1024
PARTS = 4
LEVELS = 8

VMEM = pl.BlockSpec(memory_space=pltpu.VMEM)
SMEM = pl.BlockSpec(memory_space=pltpu.SMEM)
HBM = pl.BlockSpec(memory_space=pltpu.HBM)


def call(kernel, ins, outs, scratch, flops):
    return pl.pallas_call(
        kernel,
        out_shape=[jax.ShapeDtypeStruct(s, jnp.float32) if isinstance(s, tuple) else s for s in outs],
        in_specs=ins,
        out_specs=[VMEM] * len(outs),
        scratch_shapes=[pltpu.VMEM(s, jnp.float32) if isinstance(s, tuple) else s for s in scratch],
        compiler_params=pltpu.CompilerParams(vmem_limit_bytes=LIMIT),
        cost_estimate=pl.CostEstimate(flops=flops, bytes_accessed=1 << 20, transcendentals=0),
    )


def pack_kernel(c_hbm, wx_hbm, wy_hbm, *refs):
    small, (own_ref, yl_ref, yr_ref), kept, (in_ref, sems, small_sems) = refs[:4], refs[4:7], refs[7:11], refs[11:]
    depth, rows, width = c_hbm.shape
    half, strip, part = rows // 2, HSTEPS, depth // PARTS
    copies = []
    for a, ref in enumerate((c_hbm, wx_hbm, wy_hbm)):
        for q in range(PARTS):
            at = pl.ds(q * part, part)
            copies.append(pltpu.make_async_copy(ref.at[at], in_ref.at[a, at], sems.at[a * PARTS + q]))
            copies[-1].start()
    others = [pltpu.make_async_copy(s, d, small_sems.at[i]) for i, (s, d) in enumerate(zip(small, kept))]
    for copy in others:
        copy.start()
    lane = lax.broadcasted_iota(jnp.int32, (depth, TILE), 1) // strip
    for a in range(3):
        for q in range(PARTS):
            copies[a * PARTS + q].wait()
        left = jnp.zeros((depth, TILE), jnp.float32)
        right = left
        for x in range(rows):
            row = in_ref[a, :, x, :]
            own_ref[a, x] = row
            first, last = row[:, :TILE], row[:, width - TILE :]
            group = 2 * (x % half)
            to_left, to_right = group + 1 - x // half, group + x // half
            if to_left:
                first = pltpu.roll(first, strip * to_left, 1)
            if (to_right + 1) * strip % TILE:
                last = pltpu.roll(last, (to_right + 1) * strip % TILE, 1)
            left = jnp.where(lane == to_left, first, left)
            right = jnp.where(lane == to_right, last, right)
        yl_ref[a] = left
        yr_ref[a] = right
    for copy in others:
        copy.wait()


def send_kernel(own_ref, south_ref, north_ref, lo_ref, hi_ref, side_lo_ref, side_hi_ref):
    _, rows, depth, width = own_ref.shape
    half = rows // 2
    to_lo, to_hi = 0, 0
    for a in range(3):
        for x in range(rows):
            first, last = own_ref[a, x, :, :TILE], own_ref[a, x, :, TILE:]
            if x < half and not (a > 0 and x == half - 1):
                lo_ref[to_lo], lo_ref[to_lo + 1] = first, last
                to_lo += 2
            if x >= half and not (a == 2 and x == half):
                hi_ref[to_hi], hi_ref[to_hi + 1] = first, last
                to_hi += 2
    even = lax.broadcasted_iota(jnp.int32, (depth, TILE), 1) // HSTEPS % 2 == 0
    for a in range(3):
        south, north = south_ref[a], north_ref[a]
        low = jnp.where(even, south, north)
        high = jnp.where(even, pltpu.roll(south, TILE - HSTEPS, 1), pltpu.roll(north, HSTEPS, 1))
        side_lo_ref[a] = low
        side_hi_ref[a] = high
        lo_ref[to_lo + a] = low
        hi_ref[to_hi + a] = high


def mixing_numbers(profiles_ref, classes_ref, heights_ref, k_ref):
    total = k_ref.shape[0] - 1
    classes, heights = classes_ref[...], heights_ref[...]
    bits = [(classes & (1 << b)) != 0 for b in range(3)]
    k_ref[0] = jnp.zeros(classes.shape, jnp.float32)

    def mixing(z, _):
        table = [profiles_ref[c, z] for c in range(NCLASS)]
        for bit in bits:
            table = [jnp.where(bit, table[i + 1], table[i]) for i in range(0, len(table), 2)]
        k = table[0]
        k_ref[z + 1] = jnp.where(z < heights, CANOPY * k, k)
        return 0

    lax.fori_loop(0, total, mixing, 0, unroll=8)


def factor_kernel(profiles_ref, classes_ref, heights_ref, f_ref, h_ref, g_ref, a_ref, b_ref, w_ref,
                  k_ref, n_ref, m_ref, p_ref, q_ref, up_ref, down_ref):
    me = lax.axis_index("gz")
    depth = g_ref.shape[0]
    groups = w_ref.shape[0]
    shape = w_ref.shape[1:]
    total = depth * groups
    one = jnp.ones(shape, jnp.float32)
    mixing_numbers(profiles_ref, classes_ref, heights_ref, k_ref)

    def some(t, carry):
        n, p, up, down = carry
        low = t * LEVELS
        high = total - 1 - low
        chunk_n, chunk_p = low // depth, high // depth
        at_n = low % depth + jnp.where(chunk_n == me, 0, depth)
        at_p = high % depth + jnp.where(chunk_p == me, 0, depth)
        m, q = one, one
        for i in range(LEVELS):
            k, kb = k_ref[low + i + 1], k_ref[high - i]
            n_ref[at_n + i], m_ref[at_n + i] = n, m
            p_ref[at_p - i], q_ref[at_p - i] = p, q
            m, q = n + k * m, p + kb * q
            n, p = m + k * n, q + kb * p
            up, down = up * k, down * kb
        m, q = 1.0 / m, 1.0 / q
        up, down = up * m, down * q
        up_ref[chunk_n], down_ref[chunk_p] = up, down
        fresh = low % depth + LEVELS == depth
        return n * m, p * q, jnp.where(fresh, one, up), jnp.where(fresh, one, down)

    lax.fori_loop(0, total // LEVELS, some, (one, 1.0 + k_ref[total], one, one))

    begin = me * depth
    for i in range(depth):
        m, q = m_ref[i], q_ref[i]
        k, kb = k_ref[begin + i + 1], k_ref[begin + i]
        f_ref[i] = k * m / (n_ref[i] + k * m)
        h_ref[i] = kb * q / (p_ref[i] + kb * q)
        g_ref[i] = m * q / (n_ref[i] * q + p_ref[i] * m - m * q)
    run = one
    for i in range(depth):
        a_ref[i] = g_ref[i] * run
        run = run * f_ref[i]
    run = one
    for i in reversed(range(depth)):
        b_ref[i] = g_ref[i] * run
        run = run * h_ref[i]
    zero = jnp.zeros(shape, jnp.float32)
    run = one
    for s in reversed(range(groups)):
        below = s < me
        w_ref[s] = jnp.where(below, run, zero)
        run = jnp.where(below, run * up_ref[s], one)
    run = one
    for s in range(groups):
        above = s > me
        w_ref[s] = w_ref[s] + jnp.where(above, run, zero)
        run = jnp.where(above, run * down_ref[s], one)


def coefficients(ax, aw, ay, mask):
    south = pltpu.roll(ay, 1, 1)
    ax_up, ay_up, as_up = jnp.maximum(ax, 0.0), jnp.maximum(ay, 0.0), jnp.maximum(south, 0.0)
    ax_down, ay_down, as_down = jnp.minimum(ax, 0.0), jnp.minimum(ay, 0.0), jnp.minimum(south, 0.0)
    own = (1.0 - 4.0 * DIFFUSION) - ax_up - (ay_up - as_down)
    west = DIFFUSION
    if aw is not None:
        own = own + jnp.minimum(aw, 0.0)
        west = west + jnp.maximum(aw, 0.0)
    return own * mask, (DIFFUSION - ax_down) * mask, west * mask, (DIFFUSION - ay_down) * mask, (DIFFUSION + as_up) * mask


def substep(k_ref, r, own, east, west):
    north = pltpu.roll(own, own.shape[1] - 1, 1)
    south = pltpu.roll(own, 1, 1)
    return (k_ref[0, r] * own + k_ref[1, r] * east) + (k_ref[2, r] * west + k_ref[3, r] * north) + k_ref[4, r] * south


def with_strips(first, last, side, row):
    by = (TILE - HSTEPS - 2 * HSTEPS * row) % TILE
    return jnp.concatenate([first, last, pltpu.roll(side, by, 1) if by else side], axis=1)


def inside_mask(depth, width):
    gy, n_gy = lax.axis_index("gy"), lax.axis_size("gy")
    lane = lax.broadcasted_iota(jnp.int32, (depth, TILE), 1)
    sides = jnp.where((lane < HSTEPS) & (gy < n_gy - 1) | (lane >= TILE - HSTEPS) & (gy > 0), 1.0, 0.0)
    return jnp.concatenate([jnp.ones((depth, width), jnp.float32), sides], axis=1)


def inner_kernel(own_ref, side_lo_ref, side_hi_ref, k_ref, edge_ref, wind_ref, c_ref):
    _, rows, depth, width = own_ref.shape
    half = rows // 2
    mask = inside_mask(depth, width)

    def plane(a, x):
        side = side_lo_ref[a] if x < half else side_hi_ref[a]
        return with_strips(own_ref[a, x, :, :TILE], own_ref[a, x, :, TILE:], side, x % half)

    aw = None
    for x in range(rows):
        c_ref[0, x] = plane(0, x)
        ax = plane(1, x)
        for i, k in enumerate(coefficients(ax, aw, plane(2, x), mask)):
            k_ref[i, x] = k
        aw = ax
    wind_ref[...] = aw
    for step in range(HSTEPS):
        src = step % 2
        for i, x in enumerate((step, step + 1, rows - 2 - step, rows - 1 - step)):
            edge_ref[step, i] = c_ref[src, x]
        for x in range(step + 1, rows - 1 - step):
            c_ref[1 - src, x] = substep(k_ref, x, c_ref[src, x], c_ref[src, x + 1], c_ref[src, x - 1])


def outer_kernel(low, got_ref, inner_ref, edge_ref, wind_ref, f_ref, h_ref, g_ref, emission_ref,
                 u_ref, send_ref, c_ref, k_ref, t_ref):
    gx, me, n_gx = lax.axis_index("gx"), lax.axis_index("gz"), lax.axis_size("gx")
    depth, half, width = u_ref.shape
    strip = HSTEPS
    inside = inside_mask(depth, width)
    halo_in = inside * jnp.where(gx > 0 if low else gx < n_gx - 1, 1.0, 0.0)
    n_got = 6 * half - (2 if low else 4)

    def plane(a, r):
        at = 2 * (half * a + r - (a == 2))
        return with_strips(got_ref[at], got_ref[at + 1], got_ref[n_got + a], r)

    first = 0 if low else half + 1
    aw = plane(1, 0) if low else wind_ref[...]
    if low:
        c_ref[0, 0] = plane(0, 0)
    else:
        c_ref[0, first + strip - 1] = plane(0, strip - 1)
    for r in range(1, strip) if low else range(strip - 1):
        c_ref[0, first + r] = plane(0, r)
        ax = plane(1, r)
        for i, k in enumerate(coefficients(ax, aw, plane(2, r), halo_in)):
            k_ref[i, r] = k
        aw = ax
    if low:
        for i in range(5):
            k = inner_ref[i, 0]
            if i == 0:
                k = k + jnp.minimum(aw, 0.0) * inside
            if i == 2:
                k = k + jnp.maximum(aw, 0.0) * inside
            k_ref[i, strip] = k

    for step in range(1, strip + 1):
        src = (step - 1) % 2
        reach = strip - 1 + step if low else half + 1 - step

        def at(q):
            if low and q >= reach:
                return edge_ref[step - 1, q - reach]
            if not low and q <= reach:
                return edge_ref[step - 1, q - reach + 3]
            return c_ref[src, q]

        for i in range(strip):
            r = (step if low else reach) + i
            if low:
                weights, row = (k_ref, r) if r <= strip else (inner_ref, r - strip)
            else:
                weights, row = (k_ref, r - first) if r >= first else (inner_ref, r + half - 1)
            new = substep(weights, row, at(r), at(r + 1), at(r - 1))
            if step < strip:
                c_ref[1 - src, r] = new
            else:
                c_ref[1 - src, r, :, :width] = new[:, :width]
    last = strip % 2
    begin = strip if low else 1

    def level(z):
        d = c_ref[last, begin : begin + half, z, :width]
        if z == 0:
            mine = emission_ref[:half] if low else emission_ref[half:]
            d = d + mine * jnp.where(me == 0, 1.0, 0.0)
        return d

    mine = pl.ds(0 if low else half, half)
    run = None
    for z in range(depth):
        d = level(z)
        run = d if z == 0 else d + f_ref[z - 1, mine] * run
        t_ref[z] = run - d
    beta = f_ref[depth - 1, mine] * run
    run = None
    for z in reversed(range(depth)):
        d = level(z)
        run = d if z == depth - 1 else d + h_ref[z + 1, mine] * run
        u_ref[z] = g_ref[z, mine] * (t_ref[z] + run)
    gamma = h_ref[0, mine] * run
    send_ref[0], send_ref[1] = beta, gamma


def finish_kernel(west_ref, east_ref, a_ref, b_ref, w_ref, got_ref, out_ref):
    me = lax.axis_index("gz")
    depth, rows, width = a_ref.shape
    groups, half = w_ref.shape[0], rows // 2
    zero = jnp.zeros((rows, width), jnp.float32)
    below, above = zero, zero
    for s in range(groups):
        below = below + jnp.where(s < me, w_ref[s] * got_ref[2 * s], zero)
        above = above + jnp.where(s > me, w_ref[s] * got_ref[2 * s + 1], zero)
    for z in range(depth):
        more = a_ref[z] * below + b_ref[z] * above
        out_ref[z, :half] = west_ref[z] + more[:half]
        out_ref[z, half:] = east_ref[z] + more[half:]


def shifted(x, axis, by):
    length = lax.axis_size(axis)
    return lax.ppermute(x, axis, [(i, i + by) for i in range(length) if 0 <= i + by < length])


def local(conc, wind_x, wind_y, profiles, classes, heights, emission):
    species, depth, rows, width = conc.shape
    groups = lax.axis_size("gz")
    half, wide = rows // 2, width + TILE
    block, pane, tile, row = (depth, rows, width), (rows, width), (depth, TILE), (depth, wide)
    n_lo, n_hi = 6 * half - 4, 6 * half - 2

    small = (profiles, classes, heights, emission[0])
    own, left, right, profiles, classes, heights, emission = call(
        pack_kernel, [HBM] * 7,
        [(3, rows, depth, width), (3, *tile), (3, *tile), *(jax.ShapeDtypeStruct(x.shape, x.dtype) for x in small)],
        [(3, *block), pltpu.SemaphoreType.DMA((3 * PARTS,)), pltpu.SemaphoreType.DMA((len(small),))], 1 << 20,
    )(*(pltpu.with_memory_space_constraint(x, pltpu.HBM) for x in (conc[0], wind_x, wind_y, *small)))
    south = shifted(right, "gy", 1)
    north = shifted(left, "gy", -1)
    lo, hi, side_lo, side_hi = call(
        send_kernel, [VMEM] * 3,
        [(n_lo + 3, *tile), (n_hi + 3, *tile), (3, *tile), (3, *tile)], [], 1 << 20
    )(own, south, north)
    west = shifted(hi, "gx", 1)
    east = shifted(lo, "gx", -1)
    weights, edge, wind = call(
        inner_kernel, [VMEM] * 3,
        [(5, rows, *row), (HSTEPS, 4, *row), row], [(2, rows, *row)], 1 << 24,
    )(own, side_lo, side_hi)
    twice = (2 * depth, rows, width)
    profiles, _ = lax.optimization_barrier((profiles, side_lo))
    f, h, g, a, b, w = call(
        factor_kernel, [SMEM, VMEM, VMEM], [block] * 5 + [(groups, *pane)],
        [(depth * groups + 1, *pane)] + [twice] * 4 + [(groups, *pane)] * 2, 1 << 24,
    )(profiles, classes, heights)
    halves = []
    for low, got in ((True, west), (False, east)):
        if not low:
            wind, _ = lax.optimization_barrier((wind, halves[0][1]))
        halves.append(call(
            functools.partial(outer_kernel, low), [VMEM] * 8,
            [(depth, half, width), (2, half, width)],
            [(2, half + HSTEPS + 1, *row), (5, HSTEPS + 1, *row), (depth, half, width)], 1 << 24,
        )(got, weights, edge, wind, f, h, g, emission))
    send = jnp.concatenate([s for _, s in halves], axis=1)
    got = lax.all_gather(send, "gz", axis=0, tiled=True)
    (out,) = call(
        finish_kernel, [VMEM] * 6, [block], [], 1 << 20
    )(*(u for u, _ in halves), a, b, w, got)
    return out[None]


def solution(mesh):
    return jax.shard_map(
        local,
        mesh=mesh,
        in_specs=(
            P(None, "gz", "gx", "gy"),
            P("gz", "gx", "gy"),
            P("gz", "gx", "gy"),
            P(),
            P("gx", "gy"),
            P("gx", "gy"),
            P(None, "gx", "gy"),
        ),
        out_specs=P(None, "gz", "gx", "gy"),
        check_vma=False,
    )
```

```python
import functools

import jax
import jax.numpy as jnp
from jax import lax
from jax.experimental import pallas as pl
from jax.experimental.pallas import tpu as pltpu
from jax.sharding import PartitionSpec as P

HSTEPS = 8
NCLASS = 8
TILE = 128
DIFFUSION = 0.05
CANOPY = 0.2
LIMIT = 8 * 1024 * 1024
PARTS = 4
LEVELS = 8

VMEM = pl.BlockSpec(memory_space=pltpu.VMEM)
SMEM = pl.BlockSpec(memory_space=pltpu.SMEM)
HBM = pl.BlockSpec(memory_space=pltpu.HBM)


def call(kernel, ins, outs, scratch, flops):
    return pl.pallas_call(
        kernel,
        out_shape=[jax.ShapeDtypeStruct(s, jnp.float32) if isinstance(s, tuple) else s for s in outs],
        in_specs=ins,
        out_specs=[VMEM] * len(outs),
        scratch_shapes=[pltpu.VMEM(s, jnp.float32) if isinstance(s, tuple) else s for s in scratch],
        compiler_params=pltpu.CompilerParams(vmem_limit_bytes=LIMIT),
        cost_estimate=pl.CostEstimate(flops=flops, bytes_accessed=1 << 20, transcendentals=0),
    )


def pack_kernel(c_hbm, wx_hbm, wy_hbm, *refs):
    small, (own_ref, yl_ref, yr_ref), kept, (in_ref, sems, small_sems) = refs[:4], refs[4:7], refs[7:11], refs[11:]
    depth, rows, width = c_hbm.shape
    half, strip, part = rows // 2, HSTEPS, depth // PARTS
    copies = []
    for a, ref in enumerate((c_hbm, wx_hbm, wy_hbm)):
        for q in range(PARTS):
            at = pl.ds(q * part, part)
            copies.append(pltpu.make_async_copy(ref.at[at], in_ref.at[a, at], sems.at[a * PARTS + q]))
            copies[-1].start()
    others = [pltpu.make_async_copy(s, d, small_sems.at[i]) for i, (s, d) in enumerate(zip(small, kept))]
    for copy in others:
        copy.start()
    lane = lax.broadcasted_iota(jnp.int32, (depth, TILE), 1) // strip
    for a in range(3):
        for q in range(PARTS):
            copies[a * PARTS + q].wait()
        left = jnp.zeros((depth, TILE), jnp.float32)
        right = left
        for x in range(rows):
            row = in_ref[a, :, x, :]
            own_ref[a, x] = row
            first, last = row[:, :TILE], row[:, width - TILE :]
            group = 2 * (x % half)
            to_left, to_right = group + 1 - x // half, group + x // half
            if to_left:
                first = pltpu.roll(first, strip * to_left, 1)
            if (to_right + 1) * strip % TILE:
                last = pltpu.roll(last, (to_right + 1) * strip % TILE, 1)
            left = jnp.where(lane == to_left, first, left)
            right = jnp.where(lane == to_right, last, right)
        yl_ref[a] = left
        yr_ref[a] = right
    for copy in others:
        copy.wait()


def send_kernel(own_ref, south_ref, north_ref, lo_ref, hi_ref, side_lo_ref, side_hi_ref):
    _, rows, depth, width = own_ref.shape
    half = rows // 2
    to_lo, to_hi = 0, 0
    for a in range(3):
        for x in range(rows):
            first, last = own_ref[a, x, :, :TILE], own_ref[a, x, :, TILE:]
            if x < half and not (a > 0 and x == half - 1):
                lo_ref[to_lo], lo_ref[to_lo + 1] = first, last
                to_lo += 2
            if x >= half and not (a == 2 and x == half):
                hi_ref[to_hi], hi_ref[to_hi + 1] = first, last
                to_hi += 2
    even = lax.broadcasted_iota(jnp.int32, (depth, TILE), 1) // HSTEPS % 2 == 0
    for a in range(3):
        south, north = south_ref[a], north_ref[a]
        low = jnp.where(even, south, north)
        high = jnp.where(even, pltpu.roll(south, TILE - HSTEPS, 1), pltpu.roll(north, HSTEPS, 1))
        side_lo_ref[a] = low
        side_hi_ref[a] = high
        lo_ref[to_lo + a] = low
        hi_ref[to_hi + a] = high


def mixing_kernel(profiles_ref, classes_ref, heights_ref, k_ref):
    total = k_ref.shape[0] - 1
    classes, heights = classes_ref[...], heights_ref[...]
    bits = [(classes & (1 << b)) != 0 for b in range(3)]
    k_ref[0] = jnp.zeros(classes.shape, jnp.float32)

    def mixing(z, _):
        table = [profiles_ref[c, z] for c in range(NCLASS)]
        for bit in bits:
            table = [jnp.where(bit, table[i + 1], table[i]) for i in range(0, len(table), 2)]
        k = table[0]
        k_ref[z + 1] = jnp.where(z < heights, CANOPY * k, k)
        return 0

    lax.fori_loop(0, total, mixing, 0, unroll=8)


def factor_kernel(k_ref, f_ref, h_ref, g_ref, a_ref, b_ref, w_ref,
                  n_ref, m_ref, p_ref, q_ref, up_ref, down_ref):
    me = lax.axis_index("gz")
    depth = g_ref.shape[0]
    groups = w_ref.shape[0]
    shape = w_ref.shape[1:]
    total = depth * groups
    one = jnp.ones(shape, jnp.float32)

    def some(t, carry):
        n, p, up, down = carry
        low = t * LEVELS
        high = total - 1 - low
        chunk_n, chunk_p = low // depth, high // depth
        at_n = low % depth + jnp.where(chunk_n == me, 0, depth)
        at_p = high % depth + jnp.where(chunk_p == me, 0, depth)
        m, q = one, one
        for i in range(LEVELS):
            k, kb = k_ref[low + i + 1], k_ref[high - i]
            n_ref[at_n + i], m_ref[at_n + i] = n, m
            p_ref[at_p - i], q_ref[at_p - i] = p, q
            m, q = n + k * m, p + kb * q
            n, p = m + k * n, q + kb * p
            up, down = up * k, down * kb
        m, q = 1.0 / m, 1.0 / q
        up, down = up * m, down * q
        up_ref[chunk_n], down_ref[chunk_p] = up, down
        fresh = low % depth + LEVELS == depth
        return n * m, p * q, jnp.where(fresh, one, up), jnp.where(fresh, one, down)

    lax.fori_loop(0, total // LEVELS, some, (one, 1.0 + k_ref[total], one, one))

    begin = me * depth
    for i in range(depth):
        m, q = m_ref[i], q_ref[i]
        k, kb = k_ref[begin + i + 1], k_ref[begin + i]
        f_ref[i] = k * m / (n_ref[i] + k * m)
        h_ref[i] = kb * q / (p_ref[i] + kb * q)
        g_ref[i] = m * q / (n_ref[i] * q + p_ref[i] * m - m * q)
    run = one
    for i in range(depth):
        a_ref[i] = g_ref[i] * run
        run = run * f_ref[i]
    run = one
    for i in reversed(range(depth)):
        b_ref[i] = g_ref[i] * run
        run = run * h_ref[i]
    zero = jnp.zeros(shape, jnp.float32)
    run = one
    for s in reversed(range(groups)):
        below = s < me
        w_ref[s] = jnp.where(below, run, zero)
        run = jnp.where(below, run * up_ref[s], one)
    run = one
    for s in range(groups):
        above = s > me
        w_ref[s] = w_ref[s] + jnp.where(above, run, zero)
        run = jnp.where(above, run * down_ref[s], one)


def coefficients(ax, aw, ay, mask):
    south = pltpu.roll(ay, 1, 1)
    ax_up, ay_up, as_up = jnp.maximum(ax, 0.0), jnp.maximum(ay, 0.0), jnp.maximum(south, 0.0)
    ax_down, ay_down, as_down = jnp.minimum(ax, 0.0), jnp.minimum(ay, 0.0), jnp.minimum(south, 0.0)
    own = (1.0 - 4.0 * DIFFUSION) - ax_up - (ay_up - as_down)
    west = DIFFUSION
    if aw is not None:
        own = own + jnp.minimum(aw, 0.0)
        west = west + jnp.maximum(aw, 0.0)
    return own * mask, (DIFFUSION - ax_down) * mask, west * mask, (DIFFUSION - ay_down) * mask, (DIFFUSION + as_up) * mask


def substep(k_ref, r, own, east, west):
    north = pltpu.roll(own, own.shape[1] - 1, 1)
    south = pltpu.roll(own, 1, 1)
    return (k_ref[0, r] * own + k_ref[1, r] * east) + (k_ref[2, r] * west + k_ref[3, r] * north) + k_ref[4, r] * south


def with_strips(first, last, side, row):
    by = (TILE - HSTEPS - 2 * HSTEPS * row) % TILE
    return jnp.concatenate([first, last, pltpu.roll(side, by, 1) if by else side], axis=1)


def inside_mask(depth, width):
    gy, n_gy = lax.axis_index("gy"), lax.axis_size("gy")
    lane = lax.broadcasted_iota(jnp.int32, (depth, TILE), 1)
    sides = jnp.where((lane < HSTEPS) & (gy < n_gy - 1) | (lane >= TILE - HSTEPS) & (gy > 0), 1.0, 0.0)
    return jnp.concatenate([jnp.ones((depth, width), jnp.float32), sides], axis=1)


def inner_kernel(own_ref, side_lo_ref, side_hi_ref, k_ref, edge_ref, wind_ref, c_ref):
    _, rows, depth, width = own_ref.shape
    half = rows // 2
    mask = inside_mask(depth, width)

    def plane(a, x):
        side = side_lo_ref[a] if x < half else side_hi_ref[a]
        return with_strips(own_ref[a, x, :, :TILE], own_ref[a, x, :, TILE:], side, x % half)

    aw = None
    for x in range(rows):
        c_ref[0, x] = plane(0, x)
        ax = plane(1, x)
        for i, k in enumerate(coefficients(ax, aw, plane(2, x), mask)):
            k_ref[i, x] = k
        aw = ax
    wind_ref[...] = aw
    for step in range(HSTEPS):
        src = step % 2
        for i, x in enumerate((step, step + 1, rows - 2 - step, rows - 1 - step)):
            edge_ref[step, i] = c_ref[src, x]
        for x in range(step + 1, rows - 1 - step):
            c_ref[1 - src, x] = substep(k_ref, x, c_ref[src, x], c_ref[src, x + 1], c_ref[src, x - 1])


def outer_kernel(low, got_ref, inner_ref, edge_ref, wind_ref, f_ref, h_ref, g_ref, emission_ref,
                 u_ref, send_ref, c_ref, k_ref, t_ref):
    gx, me, n_gx = lax.axis_index("gx"), lax.axis_index("gz"), lax.axis_size("gx")
    depth, half, width = u_ref.shape
    strip = HSTEPS
    inside = inside_mask(depth, width)
    halo_in = inside * jnp.where(gx > 0 if low else gx < n_gx - 1, 1.0, 0.0)
    n_got = 6 * half - (2 if low else 4)

    def plane(a, r):
        at = 2 * (half * a + r - (a == 2))
        return with_strips(got_ref[at], got_ref[at + 1], got_ref[n_got + a], r)

    first = 0 if low else half + 1
    aw = plane(1, 0) if low else wind_ref[...]
    if low:
        c_ref[0, 0] = plane(0, 0)
    else:
        c_ref[0, first + strip - 1] = plane(0, strip - 1)
    for r in range(1, strip) if low else range(strip - 1):
        c_ref[0, first + r] = plane(0, r)
        ax = plane(1, r)
        for i, k in enumerate(coefficients(ax, aw, plane(2, r), halo_in)):
            k_ref[i, r] = k
        aw = ax
    if low:
        for i in range(5):
            k = inner_ref[i, 0]
            if i == 0:
                k = k + jnp.minimum(aw, 0.0) * inside
            if i == 2:
                k = k + jnp.maximum(aw, 0.0) * inside
            k_ref[i, strip] = k

    for step in range(1, strip + 1):
        src = (step - 1) % 2
        reach = strip - 1 + step if low else half + 1 - step

        def at(q):
            if low and q >= reach:
                return edge_ref[step - 1, q - reach]
            if not low and q <= reach:
                return edge_ref[step - 1, q - reach + 3]
            return c_ref[src, q]

        for i in range(strip):
            r = (step if low else reach) + i
            if low:
                weights, row = (k_ref, r) if r <= strip else (inner_ref, r - strip)
            else:
                weights, row = (k_ref, r - first) if r >= first else (inner_ref, r + half - 1)
            new = substep(weights, row, at(r), at(r + 1), at(r - 1))
            if step < strip:
                c_ref[1 - src, r] = new
            else:
                c_ref[1 - src, r, :, :width] = new[:, :width]
    last = strip % 2
    begin = strip if low else 1

    def level(z):
        d = c_ref[last, begin : begin + half, z, :width]
        if z == 0:
            mine = emission_ref[:half] if low else emission_ref[half:]
            d = d + mine * jnp.where(me == 0, 1.0, 0.0)
        return d

    mine = pl.ds(0 if low else half, half)
    run = None
    for z in range(depth):
        d = level(z)
        run = d if z == 0 else d + f_ref[z - 1, mine] * run
        t_ref[z] = run - d
    beta = f_ref[depth - 1, mine] * run
    run = None
    for z in reversed(range(depth)):
        d = level(z)
        run = d if z == depth - 1 else d + h_ref[z + 1, mine] * run
        u_ref[z] = g_ref[z, mine] * (t_ref[z] + run)
    gamma = h_ref[0, mine] * run
    send_ref[0], send_ref[1] = beta, gamma


def finish_kernel(west_ref, east_ref, a_ref, b_ref, w_ref, got_ref, out_ref):
    me = lax.axis_index("gz")
    depth, rows, width = a_ref.shape
    groups, half = w_ref.shape[0], rows // 2
    zero = jnp.zeros((rows, width), jnp.float32)
    below, above = zero, zero
    for s in range(groups):
        below = below + jnp.where(s < me, w_ref[s] * got_ref[2 * s], zero)
        above = above + jnp.where(s > me, w_ref[s] * got_ref[2 * s + 1], zero)
    for z in range(depth):
        more = a_ref[z] * below + b_ref[z] * above
        out_ref[z, :half] = west_ref[z] + more[:half]
        out_ref[z, half:] = east_ref[z] + more[half:]


def shifted(x, axis, by):
    length = lax.axis_size(axis)
    return lax.ppermute(x, axis, [(i, i + by) for i in range(length) if 0 <= i + by < length])


def local(conc, wind_x, wind_y, profiles, classes, heights, emission):
    species, depth, rows, width = conc.shape
    groups = lax.axis_size("gz")
    half, wide = rows // 2, width + TILE
    block, pane, tile, row = (depth, rows, width), (rows, width), (depth, TILE), (depth, wide)
    n_lo, n_hi = 6 * half - 4, 6 * half - 2

    small = (profiles, classes, heights, emission[0])
    own, left, right, profiles, classes, heights, emission = call(
        pack_kernel, [HBM] * 7,
        [(3, rows, depth, width), (3, *tile), (3, *tile), *(jax.ShapeDtypeStruct(x.shape, x.dtype) for x in small)],
        [(3, *block), pltpu.SemaphoreType.DMA((3 * PARTS,)), pltpu.SemaphoreType.DMA((len(small),))], 1 << 20,
    )(*(pltpu.with_memory_space_constraint(x, pltpu.HBM) for x in (conc[0], wind_x, wind_y, *small)))
    south = shifted(right, "gy", 1)
    north = shifted(left, "gy", -1)
    (k,) = call(mixing_kernel, [SMEM, VMEM, VMEM], [(depth * groups + 1, *pane)], [], 1 << 24)(
        profiles, classes, heights
    )
    own, south, north, k = lax.optimization_barrier((own, south, north, k))
    lo, hi, side_lo, side_hi = call(
        send_kernel, [VMEM] * 3,
        [(n_lo + 3, *tile), (n_hi + 3, *tile), (3, *tile), (3, *tile)], [], 1 << 20
    )(own, south, north)
    west = shifted(hi, "gx", 1)
    east = shifted(lo, "gx", -1)
    weights, edge, wind = call(
        inner_kernel, [VMEM] * 3,
        [(5, rows, *row), (HSTEPS, 4, *row), row], [(2, rows, *row)], 1 << 24,
    )(own, side_lo, side_hi)
    twice = (2 * depth, rows, width)
    f, h, g, a, b, w = call(
        factor_kernel, [VMEM], [block] * 5 + [(groups, *pane)],
        [twice] * 4 + [(groups, *pane)] * 2, 1 << 24,
    )(k)
    halves = []
    for low, got in ((True, west), (False, east)):
        if not low:
            wind, _ = lax.optimization_barrier((wind, halves[0][1]))
        halves.append(call(
            functools.partial(outer_kernel, low), [VMEM] * 8,
            [(depth, half, width), (2, half, width)],
            [(2, half + HSTEPS + 1, *row), (5, HSTEPS + 1, *row), (depth, half, width)], 1 << 24,
        )(got, weights, edge, wind, f, h, g, emission))
    send = jnp.concatenate([s for _, s in halves], axis=1)
    got = lax.all_gather(send, "gz", axis=0, tiled=True)
    (out,) = call(
        finish_kernel, [VMEM] * 6, [block], [], 1 << 20
    )(*(u for u, _ in halves), a, b, w, got)
    return out[None]


def solution(mesh):
    return jax.shard_map(
        local,
        mesh=mesh,
        in_specs=(
            P(None, "gz", "gx", "gy"),
            P("gz", "gx", "gy"),
            P("gz", "gx", "gy"),
            P(),
            P("gx", "gy"),
            P("gx", "gy"),
            P(None, "gx", "gy"),
        ),
        out_specs=P(None, "gz", "gx", "gy"),
        check_vma=False,
    )
```

```python
import functools

import jax
import jax.numpy as jnp
from jax import lax
from jax.experimental import pallas as pl
from jax.experimental.pallas import tpu as pltpu
from jax.sharding import PartitionSpec as P

HSTEPS = 8
NCLASS = 8
TILE = 128
DIFFUSION = 0.05
CANOPY = 0.2
LIMIT = 8 * 1024 * 1024
PARTS = 4
LEVELS = 8

VMEM = pl.BlockSpec(memory_space=pltpu.VMEM)
SMEM = pl.BlockSpec(memory_space=pltpu.SMEM)
HBM = pl.BlockSpec(memory_space=pltpu.HBM)


def call(kernel, ins, outs, scratch, flops):
    return pl.pallas_call(
        kernel,
        out_shape=[jax.ShapeDtypeStruct(s, jnp.float32) if isinstance(s, tuple) else s for s in outs],
        in_specs=ins,
        out_specs=[VMEM] * len(outs),
        scratch_shapes=[pltpu.VMEM(s, jnp.float32) if isinstance(s, tuple) else s for s in scratch],
        compiler_params=pltpu.CompilerParams(vmem_limit_bytes=LIMIT),
        cost_estimate=pl.CostEstimate(flops=flops, bytes_accessed=1 << 20, transcendentals=0),
    )


def pack_kernel(c_hbm, wx_hbm, wy_hbm, *refs):
    small, (own_ref, yl_ref, yr_ref), kept, (in_ref, sems, small_sems) = refs[:4], refs[4:7], refs[7:11], refs[11:]
    depth, rows, width = c_hbm.shape
    half, strip, part = rows // 2, HSTEPS, depth // PARTS
    copies = []
    for a, ref in enumerate((c_hbm, wx_hbm, wy_hbm)):
        for q in range(PARTS):
            at = pl.ds(q * part, part)
            copies.append(pltpu.make_async_copy(ref.at[at], in_ref.at[a, at], sems.at[a * PARTS + q]))
            copies[-1].start()
    others = [pltpu.make_async_copy(s, d, small_sems.at[i]) for i, (s, d) in enumerate(zip(small, kept))]
    for copy in others:
        copy.start()
    lane = lax.broadcasted_iota(jnp.int32, (depth, TILE), 1) // strip
    for a in range(3):
        for q in range(PARTS):
            copies[a * PARTS + q].wait()
        left = jnp.zeros((depth, TILE), jnp.float32)
        right = left
        for x in range(rows):
            row = in_ref[a, :, x, :]
            own_ref[a, x] = row
            first, last = row[:, :TILE], row[:, width - TILE :]
            group = 2 * (x % half)
            to_left, to_right = group + 1 - x // half, group + x // half
            if to_left:
                first = pltpu.roll(first, strip * to_left, 1)
            if (to_right + 1) * strip % TILE:
                last = pltpu.roll(last, (to_right + 1) * strip % TILE, 1)
            left = jnp.where(lane == to_left, first, left)
            right = jnp.where(lane == to_right, last, right)
        yl_ref[a] = left
        yr_ref[a] = right
    for copy in others:
        copy.wait()


def send_kernel(own_ref, south_ref, north_ref, lo_ref, hi_ref, side_lo_ref, side_hi_ref):
    _, rows, depth, width = own_ref.shape
    half = rows // 2
    to_lo, to_hi = 0, 0
    for a in range(3):
        for x in range(rows):
            first, last = own_ref[a, x, :, :TILE], own_ref[a, x, :, TILE:]
            if x < half and not (a > 0 and x == half - 1):
                lo_ref[to_lo], lo_ref[to_lo + 1] = first, last
                to_lo += 2
            if x >= half and not (a == 2 and x == half):
                hi_ref[to_hi], hi_ref[to_hi + 1] = first, last
                to_hi += 2
    even = lax.broadcasted_iota(jnp.int32, (depth, TILE), 1) // HSTEPS % 2 == 0
    for a in range(3):
        south, north = south_ref[a], north_ref[a]
        low = jnp.where(even, south, north)
        high = jnp.where(even, pltpu.roll(south, TILE - HSTEPS, 1), pltpu.roll(north, HSTEPS, 1))
        side_lo_ref[a] = low
        side_hi_ref[a] = high
        lo_ref[to_lo + a] = low
        hi_ref[to_hi + a] = high


def mixing_kernel(profiles_ref, classes_ref, heights_ref, k_ref):
    total = k_ref.shape[0] - 1
    classes, heights = classes_ref[...], heights_ref[...]
    bits = [(classes & (1 << b)) != 0 for b in range(3)]
    k_ref[0] = jnp.zeros(classes.shape, jnp.float32)

    def mixing(z, _):
        table = [profiles_ref[c, z] for c in range(NCLASS)]
        for bit in bits:
            table = [jnp.where(bit, table[i + 1], table[i]) for i in range(0, len(table), 2)]
        k = table[0]
        k_ref[z + 1] = jnp.where(z < heights, CANOPY * k, k)
        return 0

    lax.fori_loop(0, total, mixing, 0, unroll=32)


def factor_kernel(k_ref, f_ref, h_ref, g_ref, a_ref, b_ref, w_ref,
                  n_ref, m_ref, p_ref, q_ref, up_ref, down_ref):
    me = lax.axis_index("gz")
    depth = g_ref.shape[0]
    groups = w_ref.shape[0]
    shape = w_ref.shape[1:]
    total = depth * groups
    one = jnp.ones(shape, jnp.float32)

    def some(t, carry):
        n, p, up, down = carry
        low = t * LEVELS
        high = total - 1 - low
        chunk_n, chunk_p = low // depth, high // depth
        at_n = low % depth + jnp.where(chunk_n == me, 0, depth)
        at_p = high % depth + jnp.where(chunk_p == me, 0, depth)
        m, q = one, one
        for i in range(LEVELS):
            k, kb = k_ref[low + i + 1], k_ref[high - i]
            n_ref[at_n + i], m_ref[at_n + i] = n, m
            p_ref[at_p - i], q_ref[at_p - i] = p, q
            m, q = n + k * m, p + kb * q
            n, p = m + k * n, q + kb * p
            up, down = up * k, down * kb
        m, q = 1.0 / m, 1.0 / q
        up, down = up * m, down * q
        up_ref[chunk_n], down_ref[chunk_p] = up, down
        fresh = low % depth + LEVELS == depth
        return n * m, p * q, jnp.where(fresh, one, up), jnp.where(fresh, one, down)

    lax.fori_loop(0, total // LEVELS, some, (one, 1.0 + k_ref[total], one, one))

    begin = me * depth
    for i in range(depth):
        m, q = m_ref[i], q_ref[i]
        k, kb = k_ref[begin + i + 1], k_ref[begin + i]
        f_ref[i] = k * m / (n_ref[i] + k * m)
        h_ref[i] = kb * q / (p_ref[i] + kb * q)
        g_ref[i] = m * q / (n_ref[i] * q + p_ref[i] * m - m * q)
    run = one
    for i in range(depth):
        a_ref[i] = g_ref[i] * run
        run = run * f_ref[i]
    run = one
    for i in reversed(range(depth)):
        b_ref[i] = g_ref[i] * run
        run = run * h_ref[i]
    zero = jnp.zeros(shape, jnp.float32)
    run = one
    for s in reversed(range(groups)):
        below = s < me
        w_ref[s] = jnp.where(below, run, zero)
        run = jnp.where(below, run * up_ref[s], one)
    run = one
    for s in range(groups):
        above = s > me
        w_ref[s] = w_ref[s] + jnp.where(above, run, zero)
        run = jnp.where(above, run * down_ref[s], one)


def coefficients(ax, aw, ay, mask):
    south = pltpu.roll(ay, 1, 1)
    ax_up, ay_up, as_up = jnp.maximum(ax, 0.0), jnp.maximum(ay, 0.0), jnp.maximum(south, 0.0)
    ax_down, ay_down, as_down = jnp.minimum(ax, 0.0), jnp.minimum(ay, 0.0), jnp.minimum(south, 0.0)
    own = (1.0 - 4.0 * DIFFUSION) - ax_up - (ay_up - as_down)
    west = DIFFUSION
    if aw is not None:
        own = own + jnp.minimum(aw, 0.0)
        west = west + jnp.maximum(aw, 0.0)
    return own * mask, (DIFFUSION - ax_down) * mask, west * mask, (DIFFUSION - ay_down) * mask, (DIFFUSION + as_up) * mask


def substep(k_ref, r, own, east, west):
    north = pltpu.roll(own, own.shape[1] - 1, 1)
    south = pltpu.roll(own, 1, 1)
    return (k_ref[0, r] * own + k_ref[1, r] * east) + (k_ref[2, r] * west + k_ref[3, r] * north) + k_ref[4, r] * south


def with_strips(first, last, side, row):
    by = (TILE - HSTEPS - 2 * HSTEPS * row) % TILE
    return jnp.concatenate([first, last, pltpu.roll(side, by, 1) if by else side], axis=1)


def inside_mask(depth, width):
    gy, n_gy = lax.axis_index("gy"), lax.axis_size("gy")
    lane = lax.broadcasted_iota(jnp.int32, (depth, TILE), 1)
    sides = jnp.where((lane < HSTEPS) & (gy < n_gy - 1) | (lane >= TILE - HSTEPS) & (gy > 0), 1.0, 0.0)
    return jnp.concatenate([jnp.ones((depth, width), jnp.float32), sides], axis=1)


def inner_kernel(own_ref, side_lo_ref, side_hi_ref, k_ref, edge_ref, wind_ref, c_ref):
    _, rows, depth, width = own_ref.shape
    half = rows // 2
    mask = inside_mask(depth, width)

    def plane(a, x):
        side = side_lo_ref[a] if x < half else side_hi_ref[a]
        return with_strips(own_ref[a, x, :, :TILE], own_ref[a, x, :, TILE:], side, x % half)

    aw = None
    for x in range(rows):
        c_ref[0, x] = plane(0, x)
        ax = plane(1, x)
        for i, k in enumerate(coefficients(ax, aw, plane(2, x), mask)):
            k_ref[i, x] = k
        aw = ax
    wind_ref[...] = aw
    for step in range(HSTEPS):
        src = step % 2
        for i, x in enumerate((step, step + 1, rows - 2 - step, rows - 1 - step)):
            edge_ref[step, i] = c_ref[src, x]
        for x in range(step + 1, rows - 1 - step):
            c_ref[1 - src, x] = substep(k_ref, x, c_ref[src, x], c_ref[src, x + 1], c_ref[src, x - 1])


def outer_kernel(low, got_ref, inner_ref, edge_ref, wind_ref, f_ref, h_ref, g_ref, emission_ref,
                 u_ref, send_ref, c_ref, k_ref, t_ref):
    gx, me, n_gx = lax.axis_index("gx"), lax.axis_index("gz"), lax.axis_size("gx")
    depth, half, width = u_ref.shape
    strip = HSTEPS
    inside = inside_mask(depth, width)
    halo_in = inside * jnp.where(gx > 0 if low else gx < n_gx - 1, 1.0, 0.0)
    n_got = 6 * half - (2 if low else 4)

    def plane(a, r):
        at = 2 * (half * a + r - (a == 2))
        return with_strips(got_ref[at], got_ref[at + 1], got_ref[n_got + a], r)

    first = 0 if low else half + 1
    aw = plane(1, 0) if low else wind_ref[...]
    if low:
        c_ref[0, 0] = plane(0, 0)
    else:
        c_ref[0, first + strip - 1] = plane(0, strip - 1)
    for r in range(1, strip) if low else range(strip - 1):
        c_ref[0, first + r] = plane(0, r)
        ax = plane(1, r)
        for i, k in enumerate(coefficients(ax, aw, plane(2, r), halo_in)):
            k_ref[i, r] = k
        aw = ax
    if low:
        for i in range(5):
            k = inner_ref[i, 0]
            if i == 0:
                k = k + jnp.minimum(aw, 0.0) * inside
            if i == 2:
                k = k + jnp.maximum(aw, 0.0) * inside
            k_ref[i, strip] = k

    for step in range(1, strip + 1):
        src = (step - 1) % 2
        reach = strip - 1 + step if low else half + 1 - step

        def at(q):
            if low and q >= reach:
                return edge_ref[step - 1, q - reach]
            if not low and q <= reach:
                return edge_ref[step - 1, q - reach + 3]
            return c_ref[src, q]

        for i in range(strip):
            r = (step if low else reach) + i
            if low:
                weights, row = (k_ref, r) if r <= strip else (inner_ref, r - strip)
            else:
                weights, row = (k_ref, r - first) if r >= first else (inner_ref, r + half - 1)
            new = substep(weights, row, at(r), at(r + 1), at(r - 1))
            if step < strip:
                c_ref[1 - src, r] = new
            else:
                c_ref[1 - src, r, :, :width] = new[:, :width]
    last = strip % 2
    begin = strip if low else 1

    def level(z):
        d = c_ref[last, begin : begin + half, z, :width]
        if z == 0:
            mine = emission_ref[:half] if low else emission_ref[half:]
            d = d + mine * jnp.where(me == 0, 1.0, 0.0)
        return d

    mine = pl.ds(0 if low else half, half)
    run = None
    for z in range(depth):
        d = level(z)
        run = d if z == 0 else d + f_ref[z - 1, mine] * run
        t_ref[z] = run - d
    beta = f_ref[depth - 1, mine] * run
    run = None
    for z in reversed(range(depth)):
        d = level(z)
        run = d if z == depth - 1 else d + h_ref[z + 1, mine] * run
        u_ref[z] = g_ref[z, mine] * (t_ref[z] + run)
    gamma = h_ref[0, mine] * run
    send_ref[0], send_ref[1] = beta, gamma


def finish_kernel(west_ref, east_ref, a_ref, b_ref, w_ref, got_ref, out_ref):
    me = lax.axis_index("gz")
    depth, rows, width = a_ref.shape
    groups, half = w_ref.shape[0], rows // 2
    zero = jnp.zeros((rows, width), jnp.float32)
    below, above = zero, zero
    for s in range(groups):
        below = below + jnp.where(s < me, w_ref[s] * got_ref[2 * s], zero)
        above = above + jnp.where(s > me, w_ref[s] * got_ref[2 * s + 1], zero)
    for z in range(depth):
        more = a_ref[z] * below + b_ref[z] * above
        out_ref[z, :half] = west_ref[z] + more[:half]
        out_ref[z, half:] = east_ref[z] + more[half:]


def shifted(x, axis, by):
    length = lax.axis_size(axis)
    return lax.ppermute(x, axis, [(i, i + by) for i in range(length) if 0 <= i + by < length])


def local(conc, wind_x, wind_y, profiles, classes, heights, emission):
    species, depth, rows, width = conc.shape
    groups = lax.axis_size("gz")
    half, wide = rows // 2, width + TILE
    block, pane, tile, row = (depth, rows, width), (rows, width), (depth, TILE), (depth, wide)
    n_lo, n_hi = 6 * half - 4, 6 * half - 2

    small = (profiles, classes, heights, emission[0])
    own, left, right, profiles, classes, heights, emission = call(
        pack_kernel, [HBM] * 7,
        [(3, rows, depth, width), (3, *tile), (3, *tile), *(jax.ShapeDtypeStruct(x.shape, x.dtype) for x in small)],
        [(3, *block), pltpu.SemaphoreType.DMA((3 * PARTS,)), pltpu.SemaphoreType.DMA((len(small),))], 1 << 20,
    )(*(pltpu.with_memory_space_constraint(x, pltpu.HBM) for x in (conc[0], wind_x, wind_y, *small)))
    south = shifted(right, "gy", 1)
    north = shifted(left, "gy", -1)
    (k,) = call(mixing_kernel, [SMEM, VMEM, VMEM], [(depth * groups + 1, *pane)], [], 1 << 24)(
        profiles, classes, heights
    )
    own, south, north, k = lax.optimization_barrier((own, south, north, k))
    lo, hi, side_lo, side_hi = call(
        send_kernel, [VMEM] * 3,
        [(n_lo + 3, *tile), (n_hi + 3, *tile), (3, *tile), (3, *tile)], [], 1 << 20
    )(own, south, north)
    west = shifted(hi, "gx", 1)
    east = shifted(lo, "gx", -1)
    weights, edge, wind = call(
        inner_kernel, [VMEM] * 3,
        [(5, rows, *row), (HSTEPS, 4, *row), row], [(2, rows, *row)], 1 << 24,
    )(own, side_lo, side_hi)
    twice = (2 * depth, rows, width)
    f, h, g, a, b, w = call(
        factor_kernel, [VMEM], [block] * 5 + [(groups, *pane)],
        [twice] * 4 + [(groups, *pane)] * 2, 1 << 24,
    )(k)
    halves = []
    for low, got in ((True, west), (False, east)):
        if not low:
            wind, _ = lax.optimization_barrier((wind, halves[0][1]))
        halves.append(call(
            functools.partial(outer_kernel, low), [VMEM] * 8,
            [(depth, half, width), (2, half, width)],
            [(2, half + HSTEPS + 1, *row), (5, HSTEPS + 1, *row), (depth, half, width)], 1 << 24,
        )(got, weights, edge, wind, f, h, g, emission))
    send = jnp.concatenate([s for _, s in halves], axis=1)
    got = lax.all_gather(send, "gz", axis=0, tiled=True)
    (out,) = call(
        finish_kernel, [VMEM] * 6, [block], [], 1 << 20
    )(*(u for u, _ in halves), a, b, w, got)
    return out[None]


def solution(mesh):
    return jax.shard_map(
        local,
        mesh=mesh,
        in_specs=(
            P(None, "gz", "gx", "gy"),
            P("gz", "gx", "gy"),
            P("gz", "gx", "gy"),
            P(),
            P("gx", "gy"),
            P("gx", "gy"),
            P(None, "gx", "gy"),
        ),
        out_specs=P(None, "gz", "gx", "gy"),
        check_vma=False,
    )
```
